128 devices in a mesh: ball: 16 (over x, y), hid: 8 (over z, core).
Axes of the slice: x: 4, y: 4, z: 4, core: 2. Of those that a mesh axis runs over, the one named last changes fastest.
Arguments:
- points: bfloat16 [131072, 256], P(('ball', 'hid')), may hold values from -6 to 6
- tree_slot: int32 [131072], P(('ball', 'hid')), may hold values from 0 to 131071, as said below
- rotated_slot: int32 [131072], P(('ball', 'hid')), may hold values from 0 to 131071, as said below
- fine_norm: float32 [2, 2, 256], replicated, may hold values from 0.1 to 1.9
- fine_qkv: bfloat16 [2, 3, 256, 256], replicated, may hold values from -2 to 2
- fine_out: bfloat16 [2, 256, 256], replicated, may hold values from -0.375 to 0.375
- fine_gate_up: bfloat16 [2, 2, 256, 1024], replicated, may hold values from -0.375 to 0.375
- fine_down: bfloat16 [2, 1024, 256], replicated, may hold values from -0.1875 to 0.1875
- pool_weight: bfloat16 [4096, 1024], P('hid'), may hold values from -0.09375 to 0.09375
- coarse_norm: float32 [2, 1024], replicated, may hold values from 0.1 to 1.9
- coarse_qkv: bfloat16 [3, 1024, 1024], P(None, None, 'hid'), may hold values from -2 to 2
- coarse_out: bfloat16 [1024, 1024], P('hid'), may hold values from -0.1875 to 0.1875
- coarse_gate_up: bfloat16 [2, 1024, 4096], P(None, None, 'hid'), may hold values from -0.1875 to 0.1875
- coarse_down: bfloat16 [4096, 1024], P('hid'), may hold values from -0.09375 to 0.09375
- unpool_weight: bfloat16 [1024, 4096], P(None, 'hid'), may hold values from -0.1875 to 0.1875
Outputs:
- joined: bfloat16 [131072, 256], P(('ball', 'hid'))
The draws below stay inside these ranges and needn't reach their ends.
Inputs may be any that keep to these rules, and one draw needn't show every extreme that they name: `tree_slot`: a permutation of the 131072 tree positions; the points of one device go to at most 16 positions of any one device and to exactly 16 positions of some device. `rotated_slot`: a permutation of the 131072 rotated positions; the points of one device go to at most 16 positions of any one device and to exactly 16 positions of some device.
All inputs are finite; a program needn't handle non-finite values.
Results may differ from the reference program's by a relative error of at most 0.033.
Values may be sent and summed in bfloat16 or wider, within the bound.
No kernel may reach another device: no remote copies, remote signals or barrier semaphores. Data moves between devices by JAX's collectives and lax.ppermute only.
A program may use at most 128 MiB of HBM per device.

```python
import math
import jax
import jax.numpy as jnp
from jax import lax

C = 256
FH = 1024
FHEADS = 8
BALL = 256
POOL = 16
CC = 1024
CH = 4096
CHEADS = 16
CBALL = 256
PTS_DEV = 1024
NPTS = 131072
N_BALL = 16
N_HID = 8


def route_law(key):
    device_count = N_BALL * N_HID
    mean_rows = PTS_DEV // device_count
    labels = jax.random.permutation(jax.random.fold_in(key, 1), device_count).astype(jnp.int32)
    ranking = jax.random.permutation(jax.random.fold_in(key, 2), device_count)
    counts = jnp.where(ranking < device_count // 4, 2 * mean_rows, jnp.where(ranking < device_count // 2, 0, mean_rows)).astype(jnp.int32)
    offset_of_row = jnp.repeat(jnp.arange(device_count, dtype=jnp.int32), counts, total_repeat_length=PTS_DEV)
    inverse_label = jnp.zeros((device_count,), jnp.int32).at[labels].set(jnp.arange(device_count, dtype=jnp.int32))
    source_shuffle = jax.vmap(lambda subkey: jax.random.permutation(subkey, PTS_DEV))(jax.random.split(jax.random.fold_in(key, 3), device_count)).astype(jnp.int32)
    target_shuffle = jax.vmap(lambda subkey: jax.random.permutation(subkey, PTS_DEV))(jax.random.split(jax.random.fold_in(key, 4), device_count)).astype(jnp.int32)
    destination = inverse_label[(labels[:, None] + offset_of_row[source_shuffle]) % device_count]
    inside = target_shuffle[destination, source_shuffle]
    return (destination * PTS_DEV + inside).reshape(-1).astype(jnp.int32)


def draw_tree_slot(key, part):
    return route_law(jax.random.fold_in(key, 101))


def draw_rotated_slot(key, part):
    return route_law(jax.random.fold_in(key, 202))


def projection_parts(key, array_shape, fan_width):
    drawn_part = jax.random.normal(jax.random.fold_in(key, 11), array_shape, jnp.float32) / math.sqrt(fan_width)
    return drawn_part


def draw_fine_qkv(key, part):
    drawn_part = projection_parts(key, (2, 3, C, C), C)
    return jnp.clip(drawn_part, -2.0, 2.0).astype(jnp.bfloat16)


def draw_coarse_qkv(key, part):
    drawn_part = projection_parts(key, (3, CC, CC), CC)
    return jnp.clip(drawn_part, -2.0, 2.0).astype(jnp.bfloat16)


def block_levels(own_key, dims, pieces, low, top_value):
    def one(axis_at, parts):
        heights = jax.random.uniform(jax.random.fold_in(jax.random.fold_in(own_key, 6), axis_at), (parts,), jnp.float32, low / len(pieces), top_value / len(pieces))
        return jnp.repeat(jnp.exp(heights), dims[axis_at] // parts).reshape((-1,) + (1,) * (len(dims) - axis_at - 1))

    level = one(*pieces[0])
    for cut in pieces[1:]:
        level = level * one(*cut)
    return level


def gaussian(own_key, extent, deviation, limit, pieces=(), kind=jnp.bfloat16):
    entries = jax.random.normal(own_key, extent, jnp.float32) * deviation
    if len(pieces) > 0:
        entries = block_levels(own_key, extent, pieces, -0.22, 0.18) * entries
    return jnp.clip(entries, min=-limit, max=limit).astype(kind)


def setup_inputs(seed: int = 0) -> dict:
    key_of = jax.random.split(jax.random.key(seed), 16)
    points = gaussian(key_of[0], (NPTS, C), 1.0, 6.0, ((0, 128),))
    tree_slot = draw_tree_slot(jax.random.fold_in(key_of[15], 71), 0)
    rotated_slot = draw_rotated_slot(jax.random.fold_in(key_of[15], 71), 0)
    fine_norm = jnp.clip(1.0 + 0.18 * jax.random.normal(key_of[3], (2, 2, C), jnp.float32), 0.1, 1.9)
    fine_qkv = draw_fine_qkv(jax.random.fold_in(key_of[15], 71), 0)
    fine_out = gaussian(key_of[5], (2, C, C), C ** -0.5, 0.375)
    fine_gate_up = gaussian(key_of[6], (2, 2, C, FH), C ** -0.5, 0.375)
    fine_down = gaussian(key_of[7], (2, FH, C), FH ** -0.5, 0.1875)
    pool_weight = gaussian(key_of[8], (POOL * C, CC), (POOL * C) ** -0.5, 0.09375, ((0, 8),))
    coarse_norm = jnp.clip(1.0 + 0.18 * jax.random.normal(key_of[9], (2, CC), jnp.float32), 0.1, 1.9)
    coarse_qkv = draw_coarse_qkv(jax.random.fold_in(key_of[15], 71), 0)
    coarse_out = gaussian(key_of[11], (CC, CC), CC ** -0.5, 0.1875, ((0, 8),))
    coarse_gate_up = gaussian(key_of[12], (2, CC, CH), CC ** -0.5, 0.1875, ((2, 8),))
    coarse_down = gaussian(key_of[13], (CH, CC), CH ** -0.5, 0.09375, ((0, 8),))
    unpool_weight = gaussian(key_of[14], (CC, POOL * C), CC ** -0.5, 0.1875, ((1, 8),))
    return dict(points=points, tree_slot=tree_slot, rotated_slot=rotated_slot, fine_norm=fine_norm, fine_qkv=fine_qkv, fine_out=fine_out, fine_gate_up=fine_gate_up, fine_down=fine_down, pool_weight=pool_weight, coarse_norm=coarse_norm, coarse_qkv=coarse_qkv, coarse_out=coarse_out, coarse_gate_up=coarse_gate_up, coarse_down=coarse_down, unpool_weight=unpool_weight)


epsilon = 1e-06

def rms_scale(values, gain):
    widened = values.astype(jnp.float32)
    mean_square = lax.optimization_barrier(jnp.mean(widened * widened, axis=-1, keepdims=True))
    return (widened * lax.rsqrt(mean_square + epsilon) * gain).astype(jnp.bfloat16)

def project(normed, weights):
    stacked = jnp.stack([jnp.dot(normed, weights[index_part], preferred_element_type=jnp.float32) for index_part in range(3)])
    return lax.optimization_barrier(stacked.astype(jnp.bfloat16))

def ball_attention(projected, head_size, ball_size):
    row_count = projected.shape[1]
    width_all = projected.shape[2]
    head_count = width_all // head_size
    shaped = jnp.transpose(projected.reshape(3, row_count // ball_size, ball_size, width_all), (1, 0, 2, 3))

    def one_ball(triple):
        widened = triple.astype(jnp.float32).reshape(3, ball_size, head_count, head_size)
        scores = jnp.einsum('qhd,khd->hqk', widened[0], widened[1]) / math.sqrt(head_size)
        weights = lax.optimization_barrier(jax.nn.softmax(scores, axis=-1).astype(jnp.bfloat16))
        mixed = jnp.einsum('hqk,khd->qhd', weights.astype(jnp.float32), widened[2])
        return mixed.reshape(ball_size, width_all).astype(jnp.bfloat16)
    return lax.map(one_ball, shaped).reshape(row_count, width_all)

def fine_block(states, block_gains, qkv_weight, out_weight, gate_up_weight, down_weight):
    projected = project(rms_scale(states, block_gains[0]), qkv_weight)
    mixed = ball_attention(projected, C // FHEADS, BALL)
    attended = (states.astype(jnp.float32) + jnp.dot(mixed, out_weight, preferred_element_type=jnp.float32)).astype(jnp.bfloat16)
    normed = rms_scale(attended, block_gains[1])
    gate_value = jnp.dot(normed, gate_up_weight[0], preferred_element_type=jnp.float32)
    upward = jnp.dot(normed, gate_up_weight[1], preferred_element_type=jnp.float32)
    hidden = (jax.nn.silu(gate_value) * upward).astype(jnp.bfloat16)
    return (attended.astype(jnp.float32) + jnp.dot(hidden, down_weight, preferred_element_type=jnp.float32)).astype(jnp.bfloat16)

def split_sum(left_side, right_side):
    row_count = left_side.shape[0]
    left_parts = left_side.astype(jnp.float32).reshape(row_count, N_HID, -1)
    right_parts = right_side.astype(jnp.float32).reshape(N_HID, -1, right_side.shape[1])
    partial_value = lax.optimization_barrier(jnp.einsum('nhc,hcd->nhd', left_parts, right_parts).astype(jnp.bfloat16))
    return lax.optimization_barrier(jnp.sum(partial_value.astype(jnp.float32), axis=1))

def reference(points, tree_slot, rotated_slot, fine_norm, fine_qkv, fine_out, fine_gate_up, fine_down, pool_weight, coarse_norm, coarse_qkv, coarse_out, coarse_gate_up, coarse_down, unpool_weight):
    ordered = jnp.zeros_like(points).at[tree_slot].set(points)
    block_one = fine_block(ordered, fine_norm[0], fine_qkv[0], fine_out[0], fine_gate_up[0], fine_down[0])
    rotated = jnp.zeros_like(block_one).at[rotated_slot].set(block_one)
    block_two = fine_block(rotated, fine_norm[1], fine_qkv[1], fine_out[1], fine_gate_up[1], fine_down[1])[rotated_slot]
    grouped = block_two.reshape(-1, POOL * C)
    coarse = jnp.dot(grouped, pool_weight, preferred_element_type=jnp.float32).astype(jnp.bfloat16)
    projected = project(rms_scale(coarse, coarse_norm[0]), coarse_qkv)
    mixed = ball_attention(projected, CC // CHEADS, CBALL)
    coarse_mid = (coarse.astype(jnp.float32) + split_sum(mixed, coarse_out)).astype(jnp.bfloat16)
    normed = rms_scale(coarse_mid, coarse_norm[1])
    gate_value = jnp.dot(normed, coarse_gate_up[0], preferred_element_type=jnp.float32)
    upward = jnp.dot(normed, coarse_gate_up[1], preferred_element_type=jnp.float32)
    hidden = (jax.nn.silu(gate_value) * upward).astype(jnp.bfloat16)
    coarse_done = (coarse_mid.astype(jnp.float32) + split_sum(hidden, coarse_down)).astype(jnp.bfloat16)
    unpooled = jnp.dot(coarse_done, unpool_weight, preferred_element_type=jnp.float32).astype(jnp.bfloat16)
    return (block_two.astype(jnp.float32) + unpooled.reshape(block_two.shape).astype(jnp.float32)).astype(jnp.bfloat16)
```

```python
import functools
import math

import jax
import jax.numpy as jnp
from jax import lax
from jax.experimental import pallas as pl
from jax.experimental.pallas import tpu as pltpu
from jax.sharding import Mesh
from jax.sharding import PartitionSpec as P

F32 = jnp.float32
BF16 = jnp.bfloat16
I32 = jnp.int32

C = 256
FH = 1024
FHEADS = 8
BALL = 256
POOL = 16
CC = 1024
N_DEV = 128
CAP = 16
PTS = 1024
SLOTS = N_DEV * CAP
CROWS = PTS // POOL
N_BALL = 16
N_Z = 4
N_HID = 8
EPS = 1e-06
LOG2E = 1.4426950408889634
ALL = ("ball", "z", "core")
VMEM_LIMIT = 56 * 2**20

NT = (((1,), (1,)), ((), ()))


def params():
    return pltpu.CompilerParams(vmem_limit_bytes=VMEM_LIMIT)


def iota(shape, dim):
    return lax.broadcasted_iota(I32, shape, dim)


def onehot(mask):
    return jnp.where(mask, 1.0, 0.0).astype(BF16)


def mm(a, b):
    return jnp.dot(a, b, preferred_element_type=F32)


def mm_nt(a, b):
    return lax.dot_general(a, b, NT, preferred_element_type=F32)


def rms(values, gain):
    mean_square = jnp.mean(values * values, axis=-1, keepdims=True)
    return (values * lax.rsqrt(mean_square + EPS) * gain).astype(BF16)


def silu(v):
    return 0.5 * v * (1.0 + jnp.tanh(0.5 * v))


def prep_kernel(points, tree, rot, send, place, slots):
    upper = onehot(iota((PTS, PTS), 0) < iota((PTS, PTS), 1))
    device = iota((N_DEV, PTS), 0)
    placed = jnp.zeros((N_DEV, N_DEV), F32)
    for which, ref in ((0, tree), (1, rot)):
        target = ref[...]
        owner = target >> 10
        within = (target & (PTS - 1)) + 1
        match = jnp.where(device == owner, 1.0, 0.0)
        match_16 = match.astype(BF16)
        before = mm(match_16, upper)
        rank = jnp.sum(match * before, axis=0, keepdims=True).astype(I32)
        slots[which : which + 1, :] = owner * CAP + rank
        column = device - 2 * CAP * which
        high = (within >> 5).astype(F32)
        low = (within & 31).astype(F32)
        spread = jnp.where(
            column == rank, high, jnp.where(column == rank + CAP, low, 0.0)
        ).astype(BF16)
        placed = placed + mm_nt(match_16, spread)
    place[...] = placed
    pack(slots[0:1, :], points, send)


def pack(slot_row, source, send):
    for chunk in range(SLOTS // 256):
        pick = onehot(iota((256, PTS), 0) + chunk * 256 == slot_row)
        send[chunk * 256 : (chunk + 1) * 256, :] = mm(pick, source[...]).astype(BF16)


def fine_ball(x_16, gains, qkv, out, gate_up, down):
    x = x_16.astype(F32)
    normed = rms(x, gains[0, 0:1, :])
    q = mm(normed, qkv[0, 0]).astype(BF16)
    k = mm(normed, qkv[0, 1]).astype(BF16)
    v = mm(normed, qkv[0, 2]).astype(BF16)
    width = C // FHEADS
    head_of = iota((BALL, C), 1) // width
    scale = LOG2E / math.sqrt(width)
    mixed = jnp.zeros((BALL, C), F32)
    inverse = jnp.zeros((BALL, C), F32)
    zero = jnp.zeros((BALL, C), BF16)
    for head in range(FHEADS):
        mine = head_of == head
        scores = mm_nt(q, jnp.where(mine, k, zero))
        top = jnp.max(scores, axis=-1, keepdims=True)
        weights = jnp.exp2((scores - top) * scale)
        total = jnp.sum(weights, axis=-1, keepdims=True)
        mixed = mixed + mm(weights.astype(BF16), jnp.where(mine, v, zero))
        inverse = jnp.where(mine, 1.0 / total, inverse)
    mixed = (mixed * inverse).astype(BF16)
    attended = (x + mm(mixed, out[0])).astype(BF16).astype(F32)
    normed = rms(attended, gains[0, 1:2, :])
    hidden = (silu(mm(normed, gate_up[0, 0])) * mm(normed, gate_up[0, 1])).astype(BF16)
    return (attended + mm(hidden, down[0])).astype(BF16)


def fine_kernel(which, rows, place, slots, gains, qkv, out, gate_up, down, send, place_row, states):
    base = 2 * CAP * which
    got = place[...]
    got_t = jnp.transpose(got)[base : base + 2 * CAP].astype(BF16)
    source = onehot(iota((N_DEV, SLOTS), 0) == (iota((N_DEV, SLOTS), 1) >> 4))
    spread = mm(got_t, source)
    row = iota((2 * CAP, SLOTS), 0)
    lane = iota((2 * CAP, SLOTS), 1)
    factor = jnp.where((row & 15) == (lane & 15), jnp.where(row < CAP, 32.0, 1.0), 0.0)
    place_row[0:1, :] = jnp.sum(spread * factor, axis=0, keepdims=True).astype(I32) - 1

    def one_ball(ball, carry):
        start = pl.multiple_of(ball * BALL, BALL)
        pick = onehot(iota((BALL, SLOTS), 0) + ball * BALL == place_row[0:1, :])
        x = mm(pick, rows[...]).astype(BF16)
        states[pl.ds(start, BALL), :] = fine_ball(x, gains, qkv, out, gate_up, down)
        return carry

    lax.fori_loop(0, PTS // BALL, one_ball, 0)

    if which == 0:
        pack(slots[1:2, :], states, send)
        return
    got_16 = got.astype(BF16)
    for chunk in range(SLOTS // 256):
        slot = iota((256, N_DEV), 0) + chunk * 256
        col = iota((256, N_DEV), 1)
        spread = mm(onehot(col == (slot >> 4)), got_16)
        inside = col - base
        hit = ((inside & 15) == (slot & 15)) & (inside >= 0) & (inside < 2 * CAP)
        factor = jnp.where(hit, jnp.where(inside < CAP, 32.0, 1.0), 0.0)
        at = jnp.sum(spread * factor, axis=1, keepdims=True).astype(I32) - 1
        pick = onehot(iota((256, PTS), 1) == at)
        send[chunk * 256 : (chunk + 1) * 256, :] = mm(pick, states[...]).astype(BF16)


def pool_kernel(returned, slots, pool, block_two, coarse, total):
    step = pl.program_id(0)
    slot = slots[1:2, :]
    high = (slot >> 5).astype(F32)
    low = (slot & 31).astype(F32)
    row = iota((8, PTS), 0)
    digits = jnp.where(row == 0, high, jnp.where(row == 1, low, 0.0)).astype(BF16)
    child = iota((128, PTS), 0)
    order = onehot(iota((128, PTS), 1) == POOL * (child & 63) + 2 * step + (child >> 6))
    found = mm_nt(order, digits)
    at = (found[:, 0:1] * 32.0 + found[:, 1:2]).astype(I32)
    pick = onehot(iota((128, SLOTS), 1) == at)
    two = mm(pick, returned[...]).astype(BF16)
    block_two[...] = two
    part = mm(two[:CROWS], pool[0, :C]) + mm(two[CROWS:], pool[0, C:])

    @pl.when(step == 0)
    def _():
        total[...] = part

    @pl.when(step > 0)
    def _():
        total[...] += part

    @pl.when(step == N_HID - 1)
    def _():
        coarse[...] = total[...].astype(BF16)


def attn_kernel(own, other_z, pair, gains, qkv, out, mid, normed_mid, keys, total):
    step = pl.program_id(0)

    @pl.when(step == 0)
    def _():
        gain = gains[0:1, :]
        keys[0:64, :] = rms(own[...].astype(F32), gain)
        keys[64:128, :] = rms(other_z[...].astype(F32), gain)
        keys[128:256, :] = rms(pair[...].astype(F32), gain)
        total[...] = own[...].astype(F32)

    q = mm(keys[0:64, :], qkv[0, 0]).astype(BF16)
    k = mm(keys[...], qkv[0, 1]).astype(BF16)
    v = mm(keys[...], qkv[0, 2]).astype(BF16)
    head_of = iota((BALL, 128), 1) // 64
    scale = LOG2E / math.sqrt(64)
    mixed = jnp.zeros((CROWS, 128), F32)
    inverse = jnp.zeros((CROWS, 128), F32)
    zero = jnp.zeros((BALL, 128), BF16)
    for head in range(2):
        mine = head_of == head
        scores = mm_nt(q, jnp.where(mine, k, zero))
        top = jnp.max(scores, axis=-1, keepdims=True)
        weights = jnp.exp2((scores - top) * scale)
        sums = jnp.sum(weights, axis=-1, keepdims=True)
        mixed = mixed + mm(weights.astype(BF16), jnp.where(mine, v, zero))
        inverse = jnp.where(mine[:CROWS], 1.0 / sums, inverse)
    mixed = (mixed * inverse).astype(BF16)
    total[...] += mm(mixed, out[0])

    @pl.when(step == N_HID - 1)
    def _():
        done = total[...].astype(BF16)
        mid[...] = done
        normed_mid[...] = rms(done.astype(F32), gains[1:2, :])


def mlp_kernel(own, pair, weights, kept, sent, total):
    step = pl.program_id(0)
    rows = jnp.concatenate([own[...], pair[...]], axis=0)
    gate = mm(rows, weights[:, 0, 0, :64, :].reshape(CC, 512))
    up = mm(rows, weights[:, 0, 1, :64, :].reshape(CC, 512))
    hidden = (silu(gate) * up).astype(BF16)
    left = mm(hidden, weights[:, 0, 0, 64:, :].reshape(512, 512))
    right = mm(hidden, weights[:, 0, 1, 64:, :].reshape(512, 512))

    @pl.when(step == 0)
    def _():
        total[:, :512] = left
        total[:, 512:] = right

    @pl.when(step > 0)
    def _():
        total[:, :512] += left
        total[:, 512:] += right

    @pl.when(step == N_Z - 1)
    def _():
        kept[...] = total[:CROWS, :]
        sent[...] = total[CROWS:, :].astype(BF16)


def unpool_kernel(mid, kept, got, block_two, unpool, joined, done, children):
    step = pl.program_id(0)

    @pl.when(step == 0)
    def _():
        done[...] = (mid[...].astype(F32) + kept[...] + got[...].astype(F32)).astype(BF16)

    spread = mm(done[...], unpool[0]).astype(BF16).astype(F32)
    start = pl.multiple_of(step * 128, 128)
    two = block_two[...].astype(F32)
    children[pl.ds(start, CROWS), :] = (two[:CROWS] + spread[:, :C]).astype(BF16)
    children[pl.ds(start + CROWS, CROWS), :] = (two[CROWS:] + spread[:, C:]).astype(BF16)

    @pl.when(step == N_HID - 1)
    def _():
        for chunk in range(4):
            point = iota((256, PTS), 0) + chunk * 256
            child = iota((256, PTS), 1)
            order = onehot(point == POOL * (child & 63) + (child >> 6))
            joined[chunk * 256 : (chunk + 1) * 256, :] = mm(order, children[...]).astype(BF16)


def shape(dims, dtype):
    return jax.ShapeDtypeStruct(dims, dtype)


def whole(dims):
    zeros = (0,) * len(dims)
    return pl.BlockSpec(dims, lambda *_: zeros)


def layer(dims, which):
    index = (which,) + (0,) * (len(dims) - 1)
    return pl.BlockSpec((1,) + dims[1:], lambda *_: index)


def along(dims):
    rest = (0,) * (len(dims) - 1)
    return pl.BlockSpec((1,) + dims[1:], lambda i: (i,) + rest)


def exchange(values):
    return lax.all_to_all(values, ALL, split_axis=0, concat_axis=0, tiled=True)


def other_core(values):
    return lax.ppermute(values, "core", [(0, 1), (1, 0)])


def other_z(values):
    return lax.ppermute(values, "z", [(0, 1), (1, 0), (2, 3), (3, 2)])


def fine(which, rows, place, slots, norm, qkv, out, gate_up, down):
    return pl.pallas_call(
        functools.partial(fine_kernel, which),
        grid=(1,),
        out_shape=shape((SLOTS, C), BF16),
        in_specs=[
            whole((SLOTS, C)),
            whole((N_DEV, N_DEV)),
            whole((2, PTS)),
            layer(norm.shape, which),
            layer(qkv.shape, which),
            layer(out.shape, which),
            layer(gate_up.shape, which),
            layer(down.shape, which),
        ],
        out_specs=whole((SLOTS, C)),
        scratch_shapes=[pltpu.VMEM((8, SLOTS), I32), pltpu.VMEM((PTS, C), BF16)],
        compiler_params=params(),
        cost_estimate=pl.CostEstimate(flops=8 * 10**9, bytes_accessed=4 * 2**20, transcendentals=0),
        name=f"fine_block_{which}",
    )(rows, place, slots, norm, qkv, out, gate_up, down)


def body(
    points,
    tree_slot,
    rotated_slot,
    fine_norm,
    fine_qkv,
    fine_out,
    fine_gate_up,
    fine_down,
    pool_weight,
    coarse_norm,
    coarse_qkv,
    coarse_out,
    coarse_gate_up,
    coarse_down,
    unpool_weight,
):
    hid = ("z", "core")
    pool_out = lax.all_gather(jnp.concatenate([pool_weight, coarse_out], axis=0), hid)
    at_ball = lax.axis_index("ball")
    gate_slice = lax.dynamic_slice_in_dim(coarse_gate_up, at_ball * 64, 64, axis=1)
    down_slice = lax.dynamic_slice_in_dim(coarse_down, at_ball * 32, 32, axis=0)
    mlp_slice = jnp.concatenate(
        [gate_slice, jnp.stack([down_slice[:, :512], down_slice[:, 512:]])], axis=1
    )
    mlp_weights = lax.all_gather(lax.all_gather(mlp_slice, "z"), "ball")
    qkv_all = lax.all_gather(coarse_qkv, hid)
    unpool_all = lax.all_gather(unpool_weight, hid)

    send, place, slots = pl.pallas_call(
        prep_kernel,
        out_shape=(shape((SLOTS, C), BF16), shape((N_DEV, N_DEV), F32), shape((2, PTS), I32)),
        compiler_params=params(),
        name="prep",
    )(points, tree_slot.reshape(1, PTS), rotated_slot.reshape(1, PTS))
    rows = exchange(send)
    place = exchange(place)
    fine_weights = (fine_norm, fine_qkv, fine_out, fine_gate_up, fine_down)
    rows = exchange(fine(0, rows, place, slots, *fine_weights))
    returned = exchange(fine(1, rows, place, slots, *fine_weights))

    block_two, coarse = pl.pallas_call(
        pool_kernel,
        grid=(N_HID,),
        out_shape=(shape((PTS, C), BF16), shape((CROWS, CC), BF16)),
        in_specs=[
            whole((SLOTS, C)),
            whole((2, PTS)),
            pl.BlockSpec((1, 512, CC), lambda i: (i, 0, 0)),
        ],
        out_specs=(pl.BlockSpec((128, C), lambda i: (i, 0)), whole((CROWS, CC))),
        scratch_shapes=[pltpu.VMEM((CROWS, CC), F32)],
        compiler_params=params(),
        name="pool",
    )(returned, slots, pool_out)

    from_z = other_z(coarse)
    from_pair = other_core(jnp.concatenate([coarse, from_z], axis=0))

    mid, normed = pl.pallas_call(
        attn_kernel,
        grid=(N_HID,),
        out_shape=(shape((CROWS, CC), BF16), shape((CROWS, CC), BF16)),
        in_specs=[
            whole((CROWS, CC)),
            whole((CROWS, CC)),
            whole((2 * CROWS, CC)),
            whole((2, CC)),
            along((N_HID, 3, CC, 128)),
            pl.BlockSpec((1, 128, CC), lambda i: (i, 4, 0)),
        ],
        out_specs=(whole((CROWS, CC)), whole((CROWS, CC))),
        scratch_shapes=[pltpu.VMEM((4 * CROWS, CC), BF16), pltpu.VMEM((CROWS, CC), F32)],
        compiler_params=params(),
        name="attn",
    )(coarse, from_z, from_pair, coarse_norm, qkv_all, pool_out)

    kept, sent = pl.pallas_call(
        mlp_kernel,
        grid=(N_Z,),
        out_shape=(shape((CROWS, CC), F32), shape((CROWS, CC), BF16)),
        in_specs=[
            whole((CROWS, CC)),
            whole((CROWS, CC)),
            pl.BlockSpec((N_BALL, 1, 2, 96, 512), lambda i: (0, i, 0, 0, 0)),
        ],
        out_specs=(whole((CROWS, CC)), whole((CROWS, CC))),
        scratch_shapes=[pltpu.VMEM((2 * CROWS, CC), F32)],
        compiler_params=params(),
        name="mlp",
    )(normed, other_core(normed), mlp_weights)

    return pl.pallas_call(
        unpool_kernel,
        grid=(N_HID,),
        out_shape=shape((PTS, C), BF16),
        in_specs=[
            whole((CROWS, CC)),
            whole((CROWS, CC)),
            whole((CROWS, CC)),
            pl.BlockSpec((128, C), lambda i: (i, 0)),
            along((N_HID, CC, 512)),
        ],
        out_specs=whole((PTS, C)),
        scratch_shapes=[pltpu.VMEM((CROWS, CC), BF16), pltpu.VMEM((PTS, C), BF16)],
        compiler_params=params(),
        name="unpool",
    )(mid, kept, other_core(sent), block_two, unpool_all)


def solution(mesh):
    split = Mesh(mesh.devices.reshape(N_BALL, N_Z, 2), ALL)
    hid = ("z", "core")
    placed = (
        P(ALL, None),
        P(ALL),
        P(ALL),
        P(),
        P(),
        P(),
        P(),
        P(),
        P(hid, None),
        P(),
        P(None, None, hid),
        P(hid, None),
        P(None, None, hid),
        P(hid, None),
        P(None, hid),
    )
    return jax.shard_map(
        body, mesh=split, in_specs=placed, out_specs=P(ALL, None), check_vma=False
    )
```

```python
import functools
import math

import jax
import jax.numpy as jnp
from jax import lax
from jax.experimental import pallas as pl
from jax.experimental.pallas import tpu as pltpu
from jax.sharding import Mesh
from jax.sharding import PartitionSpec as P

F32 = jnp.float32
BF16 = jnp.bfloat16
I32 = jnp.int32

C = 256
FH = 1024
FHEADS = 8
BALL = 256
POOL = 16
CC = 1024
N_DEV = 128
CAP = 16
PTS = 1024
SLOTS = N_DEV * CAP
CROWS = PTS // POOL
N_BALL = 16
N_Z = 4
N_HID = 8
EPS = 1e-06
LOG2E = 1.4426950408889634
ALL = ("ball", "z", "core")
VMEM_LIMIT = 56 * 2**20

NT = (((1,), (1,)), ((), ()))


def params():
    return pltpu.CompilerParams(vmem_limit_bytes=VMEM_LIMIT)


def iota(shape, dim):
    return lax.broadcasted_iota(I32, shape, dim)


def onehot(mask):
    return jnp.where(mask, 1.0, 0.0).astype(BF16)


def mm(a, b):
    return jnp.dot(a, b, preferred_element_type=F32)


def mm_nt(a, b):
    return lax.dot_general(a, b, NT, preferred_element_type=F32)


def rms(values, gain):
    mean_square = jnp.mean(values * values, axis=-1, keepdims=True)
    return (values * lax.rsqrt(mean_square + EPS) * gain).astype(BF16)


def silu(v):
    return 0.5 * v * (1.0 + jnp.tanh(0.5 * v))


def slice_kernel(at_ball, gate_up, down, pool, unpool, qkv, out, piece):
    piece[0:64, :] = gate_up[0]
    piece[64:128, :] = gate_up[1]
    piece[128:160, :] = down[:, :512]
    piece[160:192, :] = down[:, 512:]
    piece[192:224, :] = pool[:, :512]
    piece[224:256, :] = pool[:, 512:]
    piece[256:320, :] = unpool[...]
    for part in range(4):
        rows = slice(16 * part, 16 * part + 16)
        lanes = slice(128 * part, 128 * part + 128)
        for which in range(3):
            piece[320 + 16 * which : 336 + 16 * which, lanes] = qkv[which, rows, :]
        piece[368:384, lanes] = out[rows, :]


def prep_kernel(points, tree, rot, send, slots):
    upper = onehot(iota((PTS, PTS), 0) < iota((PTS, PTS), 1))
    device = iota((N_DEV, PTS), 0)
    digits = []
    for which, ref in ((0, tree), (1, rot)):
        target = ref[...]
        owner = target >> 10
        within = (target & (PTS - 1)) + 1
        match = jnp.where(device == owner, 1.0, 0.0)
        before = mm(match.astype(BF16), upper)
        rank = jnp.sum(match * before, axis=0, keepdims=True).astype(I32)
        slots[which : which + 1, :] = owner * CAP + rank
        row = device - 2 * which
        high = (within >> 5).astype(F32)
        low = (within & 31).astype(F32)
        digits.append(jnp.where(row == 0, high, jnp.where(row == 1, low, 0.0)).astype(BF16))
    for chunk in range(SLOTS // 256):
        rows = slice(chunk * 256, (chunk + 1) * 256)
        slot = iota((256, PTS), 0) + chunk * 256
        tree_pick = onehot(slot == slots[0:1, :])
        rot_pick = onehot(slot == slots[1:2, :])
        send[rows, :C] = mm(tree_pick, points[...]).astype(BF16)
        send[rows, C:] = (mm_nt(tree_pick, digits[0]) + mm_nt(rot_pick, digits[1])).astype(BF16)


def pack(slot_row, source, send):
    for chunk in range(SLOTS // 256):
        pick = onehot(iota((256, PTS), 0) + chunk * 256 == slot_row)
        send[chunk * 256 : (chunk + 1) * 256, :] = mm(pick, source[...]).astype(BF16)


def fine_ball(x_16, gains, qkv, out, gate_up, down):
    x = x_16.astype(F32)
    normed = rms(x, gains[0, 0:1, :])
    q = mm(normed, qkv[0, 0]).astype(BF16)
    k = mm(normed, qkv[0, 1]).astype(BF16)
    v = mm(normed, qkv[0, 2]).astype(BF16)
    width = C // FHEADS
    head_of = iota((BALL, C), 1) // width
    scale = LOG2E / math.sqrt(width)
    mixed = jnp.zeros((BALL, C), F32)
    inverse = jnp.zeros((BALL, C), F32)
    zero = jnp.zeros((BALL, C), BF16)
    for head in range(FHEADS):
        mine = head_of == head
        scores = mm_nt(q, jnp.where(mine, k, zero))
        top = jnp.max(scores, axis=-1, keepdims=True)
        weights = jnp.exp2((scores - top) * scale)
        total = jnp.sum(weights, axis=-1, keepdims=True)
        mixed = mixed + mm(weights.astype(BF16), jnp.where(mine, v, zero))
        inverse = jnp.where(mine, 1.0 / total, inverse)
    mixed = (mixed * inverse).astype(BF16)
    attended = (x + mm(mixed, out[0])).astype(BF16).astype(F32)
    normed = rms(attended, gains[0, 1:2, :])
    hidden = (silu(mm(normed, gate_up[0, 0])) * mm(normed, gate_up[0, 1])).astype(BF16)
    return (attended + mm(hidden, down[0])).astype(BF16)


def fine_kernel(which, rows, place, slots, gains, qkv, out, gate_up, down, send, place_row, states):
    row = iota((8, N_DEV), 0)
    lane = iota((8, N_DEV), 1)
    digit = jnp.where(row == 0, jnp.where(lane == 2 * which, 32.0, 0.0), 0.0)
    digit = jnp.where((row == 0) & (lane == 2 * which + 1), 1.0, digit).astype(BF16)
    place_row[...] = mm_nt(digit, place[...]).astype(I32) - 1

    def one_ball(ball, carry):
        start = pl.multiple_of(ball * BALL, BALL)
        pick = onehot(iota((BALL, SLOTS), 0) + ball * BALL == place_row[0:1, :])
        x = mm(pick, rows[...]).astype(BF16)
        states[pl.ds(start, BALL), :] = fine_ball(x, gains, qkv, out, gate_up, down)
        return carry

    lax.fori_loop(0, PTS // BALL, one_ball, 0)

    if which == 0:
        pack(slots[1:2, :], states, send)
        return
    for chunk in range(SLOTS // 256):
        digits = place[chunk * 256 : (chunk + 1) * 256, :].astype(F32)
        at = (digits[:, 2:3] * 32.0 + digits[:, 3:4]).astype(I32) - 1
        pick = onehot(iota((256, PTS), 1) == at)
        send[chunk * 256 : (chunk + 1) * 256, :] = mm(pick, states[...]).astype(BF16)


def pool_kernel(returned, slots, pool, block_two, coarse, total):
    step = pl.program_id(0)
    slot = slots[1:2, :]
    high = (slot >> 5).astype(F32)
    low = (slot & 31).astype(F32)
    row = iota((8, PTS), 0)
    digits = jnp.where(row == 0, high, jnp.where(row == 1, low, 0.0)).astype(BF16)
    child = iota((128, PTS), 0)
    order = onehot(iota((128, PTS), 1) == POOL * (child & 63) + 2 * step + (child >> 6))
    found = mm_nt(order, digits)
    at = (found[:, 0:1] * 32.0 + found[:, 1:2]).astype(I32)
    pick = onehot(iota((128, SLOTS), 1) == at)
    two = mm(pick, returned[...]).astype(BF16)
    block_two[...] = two

    @pl.when(step == 0)
    def _():
        total[...] = jnp.zeros_like(total)

    for half in range(2):
        rows = slice(32 * half, 32 * half + 32)
        lanes = slice(512 * half, 512 * half + 512)
        weight = pool[:, 0, rows, :].reshape(512, 512)
        total[:, lanes] += mm(two[:CROWS], weight[:C]) + mm(two[CROWS:], weight[C:])

    @pl.when(step == N_HID - 1)
    def _():
        coarse[...] = total[...].astype(BF16)


def coarse_kernel(
    own, from_z, pair, gains, heads, gate, up, down, unpool, block_two, joined, keys, total, normed, out, children
):
    step = pl.program_id(0)

    @pl.when(step == 0)
    def _():
        gain = gains[0:1, :]
        keys[0:64, :] = rms(own[...].astype(F32), gain)
        keys[64:128, :] = rms(from_z[...].astype(F32), gain)
        keys[128:256, :] = rms(pair[...].astype(F32), gain)
        total[...] = own[...].astype(F32)

    @pl.when(step < N_HID)
    def _():
        def weight(which):
            rows = slice(16 * which, 16 * which + 16)
            return jnp.stack(
                [heads[:, 0, rows, 128 * part : 128 * part + 128] for part in range(4)], axis=1
            ).reshape(CC, 128)

        for ball in range(N_BALL):
            lanes = slice(128 * (ball % 8), 128 * (ball % 8) + 128)
            for part in range(4):
                top = 64 * (ball // 8) + 16 * part
                out[top : top + 16, lanes] = heads[ball, 0, 48:64, 128 * part : 128 * part + 128]

        q = mm(keys[0:64, :], weight(0)).astype(BF16)
        k = mm(keys[...], weight(1)).astype(BF16)
        v = mm(keys[...], weight(2)).astype(BF16)
        head_of = iota((BALL, 128), 1) // 64
        scale = LOG2E / math.sqrt(64)
        mixed = jnp.zeros((CROWS, 128), F32)
        inverse = jnp.zeros((CROWS, 128), F32)
        zero = jnp.zeros((BALL, 128), BF16)
        for head in range(2):
            mine = head_of == head
            scores = mm_nt(q, jnp.where(mine, k, zero))
            top = jnp.max(scores, axis=-1, keepdims=True)
            weights = jnp.exp2((scores - top) * scale)
            sums = jnp.sum(weights, axis=-1, keepdims=True)
            mixed = mixed + mm(weights.astype(BF16), jnp.where(mine, v, zero))
            inverse = jnp.where(mine[:CROWS], 1.0 / sums, inverse)
        total[...] += mm((mixed * inverse).astype(BF16), out[...])

    @pl.when(step == N_HID)
    def _():
        mid = total[...].astype(BF16).astype(F32)
        total[...] = mid
        normed[...] = rms(mid, gains[1:2, :])

    @pl.when((step >= N_HID) & (step < 2 * N_HID))
    def _():
        rows = normed[...]
        hidden = silu(mm(rows, gate[...].reshape(CC, 512))) * mm(rows, up[...].reshape(CC, 512))
        hidden = hidden.astype(BF16)
        total[:, :512] += mm(hidden, down[:, 0, :32, :].reshape(512, 512))
        total[:, 512:] += mm(hidden, down[:, 0, 32:, :].reshape(512, 512))

    @pl.when(step == 2 * N_HID)
    def _():
        normed[...] = total[...].astype(BF16)

    @pl.when(step >= 2 * N_HID)
    def _():
        spread = mm(normed[...], unpool[...].reshape(CC, 512)).astype(BF16).astype(F32)
        start = pl.multiple_of((step - 2 * N_HID) * 128, 128)
        two = block_two[...].astype(F32)
        children[pl.ds(start, CROWS), :] = (two[:CROWS] + spread[:, :C]).astype(BF16)
        children[pl.ds(start + CROWS, CROWS), :] = (two[CROWS:] + spread[:, C:]).astype(BF16)

    @pl.when(step == 3 * N_HID - 1)
    def _():
        for chunk in range(4):
            point = iota((256, PTS), 0) + chunk * 256
            child = iota((256, PTS), 1)
            order = onehot(point == POOL * (child & 63) + (child >> 6))
            joined[chunk * 256 : (chunk + 1) * 256, :] = mm(order, children[...]).astype(BF16)


def shape(dims, dtype):
    return jax.ShapeDtypeStruct(dims, dtype)


def whole(dims):
    zeros = (0,) * len(dims)
    return pl.BlockSpec(dims, lambda *_: zeros)


def layer(dims, which):
    index = (which,) + (0,) * (len(dims) - 1)
    return pl.BlockSpec((1,) + dims[1:], lambda *_: index)


def unit(which, first):
    return pl.BlockSpec(
        (N_BALL, 1, 64, 512), lambda i: (0, jnp.clip(i - first, 0, N_HID - 1), which, 0)
    )


def exchange(values):
    return lax.all_to_all(values, ALL, split_axis=0, concat_axis=0, tiled=True)


def other_core(values):
    return lax.ppermute(values, "core", [(0, 1), (1, 0)])


def other_z(values):
    return lax.ppermute(values, "z", [(0, 1), (1, 0), (2, 3), (3, 2)])


def fine(which, rows, place, slots, norm, qkv, out, gate_up, down):
    return pl.pallas_call(
        functools.partial(fine_kernel, which),
        grid=(1,),
        out_shape=shape((SLOTS, C), BF16),
        in_specs=[
            whole((SLOTS, C)),
            pl.BlockSpec((SLOTS, N_DEV), lambda i: (0, 2)),
            whole((2, PTS)),
            layer(norm.shape, which),
            layer(qkv.shape, which),
            layer(out.shape, which),
            layer(gate_up.shape, which),
            layer(down.shape, which),
        ],
        out_specs=whole((SLOTS, C)),
        scratch_shapes=[pltpu.VMEM((8, SLOTS), I32), pltpu.VMEM((PTS, C), BF16)],
        compiler_params=params(),
        cost_estimate=pl.CostEstimate(flops=8 * 10**9, bytes_accessed=4 * 2**20, transcendentals=0),
        name=f"fine_block_{which}",
    )(rows, place, slots, norm, qkv, out, gate_up, down)


def body(
    points,
    tree_slot,
    rotated_slot,
    fine_norm,
    fine_qkv,
    fine_out,
    fine_gate_up,
    fine_down,
    pool_weight,
    coarse_norm,
    coarse_qkv,
    coarse_out,
    coarse_gate_up,
    coarse_down,
    unpool_weight,
):
    piece = pl.pallas_call(
        slice_kernel,
        grid_spec=pltpu.PrefetchScalarGridSpec(
            num_scalar_prefetch=1,
            grid=(1,),
            in_specs=[
                pl.BlockSpec((2, 64, 512), lambda i, at: (0, at[0], 0)),
                pl.BlockSpec((32, CC), lambda i, at: (at[0], 0)),
                pl.BlockSpec((32, CC), lambda i, at: (at[0], 0)),
                pl.BlockSpec((64, 512), lambda i, at: (at[0], 0)),
                pl.BlockSpec((3, 64, 128), lambda i, at: (0, at[0], 0)),
                pl.BlockSpec((64, 128), lambda i, at: (at[0] // 8, at[0] % 8)),
            ],
            out_specs=pl.BlockSpec((384, 512), lambda i, at: (0, 0)),
        ),
        out_shape=shape((384, 512), BF16),
        compiler_params=params(),
        name="cut",
    )(
        lax.axis_index("ball").reshape(1),
        coarse_gate_up,
        coarse_down,
        pool_weight,
        unpool_weight,
        coarse_qkv,
        coarse_out,
    )
    weights = lax.all_gather(piece, ALL).reshape(N_BALL, N_HID, 384, 512)

    send, slots = pl.pallas_call(
        prep_kernel,
        out_shape=(shape((SLOTS, C + N_DEV), BF16), shape((2, PTS), I32)),
        compiler_params=params(),
        name="prep",
    )(points, tree_slot.reshape(1, PTS), rotated_slot.reshape(1, PTS))
    first = exchange(send)
    fine_weights = (fine_norm, fine_qkv, fine_out, fine_gate_up, fine_down)
    rows = exchange(fine(0, first, first, slots, *fine_weights))
    returned = exchange(fine(1, rows, first, slots, *fine_weights))

    block_two, coarse = pl.pallas_call(
        pool_kernel,
        grid=(N_HID,),
        out_shape=(shape((PTS, C), BF16), shape((CROWS, CC), BF16)),
        in_specs=[whole((SLOTS, C)), whole((2, PTS)), unit(3, 0)],
        out_specs=(pl.BlockSpec((128, C), lambda i: (i, 0)), whole((CROWS, CC))),
        scratch_shapes=[pltpu.VMEM((CROWS, CC), F32)],
        compiler_params=params(),
        name="pool",
    )(returned, slots, weights)

    from_z = other_z(coarse)
    from_pair = other_core(jnp.concatenate([coarse, from_z], axis=0))

    return pl.pallas_call(
        coarse_kernel,
        grid=(3 * N_HID,),
        out_shape=shape((PTS, C), BF16),
        in_specs=[
            whole((CROWS, CC)),
            whole((CROWS, CC)),
            whole((2 * CROWS, CC)),
            whole((2, CC)),
            unit(5, 0),
            unit(0, N_HID),
            unit(1, N_HID),
            unit(2, N_HID),
            unit(4, 2 * N_HID),
            pl.BlockSpec((128, C), lambda i: (jnp.clip(i - 2 * N_HID, 0, N_HID - 1), 0)),
        ],
        out_specs=whole((PTS, C)),
        scratch_shapes=[
            pltpu.VMEM((4 * CROWS, CC), BF16),
            pltpu.VMEM((CROWS, CC), F32),
            pltpu.VMEM((CROWS, CC), BF16),
            pltpu.VMEM((128, CC), BF16),
            pltpu.VMEM((PTS, C), BF16),
        ],
        compiler_params=params(),
        name="coarse",
    )(coarse, from_z, from_pair, coarse_norm, *[weights] * 5, block_two)


def solution(mesh):
    split = Mesh(mesh.devices.reshape(N_BALL, N_Z, 2), ALL)
    hid = ("z", "core")
    placed = (
        P(ALL, None),
        P(ALL),
        P(ALL),
        P(),
        P(),
        P(),
        P(),
        P(),
        P(hid, None),
        P(),
        P(None, None, hid),
        P(hid, None),
        P(None, None, hid),
        P(hid, None),
        P(None, hid),
    )
    return jax.shard_map(
        body, mesh=split, in_specs=placed, out_specs=P(ALL, None), check_vma=False
    )
```

```python
import functools
import math

import jax
import jax.numpy as jnp
from jax import lax
from jax.experimental import pallas as pl
from jax.experimental.pallas import tpu as pltpu
from jax.sharding import Mesh
from jax.sharding import PartitionSpec as P

F32 = jnp.float32
BF16 = jnp.bfloat16
I32 = jnp.int32

C = 256
FH = 1024
FHEADS = 8
BALL = 256
POOL = 16
CC = 1024
N_DEV = 128
CAP = 16
PTS = 1024
SLOTS = N_DEV * CAP
CROWS = PTS // POOL
N_BALL = 16
N_Z = 4
N_HID = 8
EPS = 1e-06
LOG2E = 1.4426950408889634
ALL = ("ball", "z", "core")
VMEM_LIMIT = 56 * 2**20

NT = (((1,), (1,)), ((), ()))


def params():
    return pltpu.CompilerParams(vmem_limit_bytes=VMEM_LIMIT)


def iota(shape, dim):
    return lax.broadcasted_iota(I32, shape, dim)


def onehot(mask):
    return jnp.where(mask, 1.0, 0.0).astype(BF16)


def mm(a, b):
    return jnp.dot(a, b, preferred_element_type=F32)


def mm_nt(a, b):
    return lax.dot_general(a, b, NT, preferred_element_type=F32)


def rms(values, gain):
    mean_square = jnp.mean(values * values, axis=-1, keepdims=True)
    return (values * lax.rsqrt(mean_square + EPS) * gain).astype(BF16)


def silu(v):
    return 0.5 * v * (1.0 + jnp.tanh(0.5 * v))


def slice_kernel(at_ball, pool, unpool, qkv, out, piece):
    piece[0:32, :] = pool[:, :512]
    piece[32:64, :] = pool[:, 512:]
    piece[64:128, :] = unpool[...]
    for part in range(4):
        rows = slice(16 * part, 16 * part + 16)
        lanes = slice(128 * part, 128 * part + 128)
        for which in range(3):
            piece[128 + 16 * which : 144 + 16 * which, lanes] = qkv[which, rows, :]
        piece[176:192, lanes] = out[rows, :]


def prep_kernel(points, tree, rot, send, slots):
    upper = onehot(iota((PTS, PTS), 0) < iota((PTS, PTS), 1))
    device = iota((N_DEV, PTS), 0)
    digits = []
    for which, ref in ((0, tree), (1, rot)):
        target = ref[...]
        owner = target >> 10
        within = (target & (PTS - 1)) + 1
        match = jnp.where(device == owner, 1.0, 0.0)
        before = mm(match.astype(BF16), upper)
        rank = jnp.sum(match * before, axis=0, keepdims=True).astype(I32)
        slots[which : which + 1, :] = owner * CAP + rank
        row = device - 2 * which
        high = (within >> 5).astype(F32)
        low = (within & 31).astype(F32)
        digits.append(jnp.where(row == 0, high, jnp.where(row == 1, low, 0.0)).astype(BF16))
    for chunk in range(SLOTS // 256):
        rows = slice(chunk * 256, (chunk + 1) * 256)
        slot = iota((256, PTS), 0) + chunk * 256
        tree_pick = onehot(slot == slots[0:1, :])
        rot_pick = onehot(slot == slots[1:2, :])
        send[rows, :C] = mm(tree_pick, points[...]).astype(BF16)
        send[rows, C:] = (mm_nt(tree_pick, digits[0]) + mm_nt(rot_pick, digits[1])).astype(BF16)


def pack(slot_row, source, send):
    for chunk in range(SLOTS // 256):
        pick = onehot(iota((256, PTS), 0) + chunk * 256 == slot_row)
        send[chunk * 256 : (chunk + 1) * 256, :] = mm(pick, source[...]).astype(BF16)


def fine_ball(x_16, gains, qkv, out, gate_up, down):
    x = x_16.astype(F32)
    normed = rms(x, gains[0, 0:1, :])
    q = mm(normed, qkv[0, 0]).astype(BF16)
    k = mm(normed, qkv[0, 1]).astype(BF16)
    v = mm(normed, qkv[0, 2]).astype(BF16)
    width = C // FHEADS
    head_of = iota((BALL, C), 1) // width
    scale = LOG2E / math.sqrt(width)
    mixed = jnp.zeros((BALL, C), F32)
    inverse = jnp.zeros((BALL, C), F32)
    zero = jnp.zeros((BALL, C), BF16)
    for head in range(FHEADS):
        mine = head_of == head
        scores = mm_nt(q, jnp.where(mine, k, zero))
        top = jnp.max(scores, axis=-1, keepdims=True)
        weights = jnp.exp2((scores - top) * scale)
        total = jnp.sum(weights, axis=-1, keepdims=True)
        mixed = mixed + mm(weights.astype(BF16), jnp.where(mine, v, zero))
        inverse = jnp.where(mine, 1.0 / total, inverse)
    mixed = (mixed * inverse).astype(BF16)
    attended = (x + mm(mixed, out[0])).astype(BF16).astype(F32)
    normed = rms(attended, gains[0, 1:2, :])
    hidden = (silu(mm(normed, gate_up[0, 0])) * mm(normed, gate_up[0, 1])).astype(BF16)
    return (attended + mm(hidden, down[0])).astype(BF16)


def fine_kernel(which, rows, place, slots, gains, qkv, out, gate_up, down, send, place_row, states):
    row = iota((8, N_DEV), 0)
    lane = iota((8, N_DEV), 1)
    digit = jnp.where(row == 0, jnp.where(lane == 2 * which, 32.0, 0.0), 0.0)
    digit = jnp.where((row == 0) & (lane == 2 * which + 1), 1.0, digit).astype(BF16)
    place_row[...] = mm_nt(digit, place[...]).astype(I32) - 1

    def one_ball(ball, carry):
        start = pl.multiple_of(ball * BALL, BALL)
        pick = onehot(iota((BALL, SLOTS), 0) + ball * BALL == place_row[0:1, :])
        x = mm(pick, rows[...]).astype(BF16)
        states[pl.ds(start, BALL), :] = fine_ball(x, gains, qkv, out, gate_up, down)
        return carry

    lax.fori_loop(0, PTS // BALL, one_ball, 0)

    if which == 0:
        pack(slots[1:2, :], states, send)
        return
    for chunk in range(SLOTS // 256):
        digits = place[chunk * 256 : (chunk + 1) * 256, :].astype(F32)
        at = (digits[:, 2:3] * 32.0 + digits[:, 3:4]).astype(I32) - 1
        pick = onehot(iota((256, PTS), 1) == at)
        send[chunk * 256 : (chunk + 1) * 256, :] = mm(pick, states[...]).astype(BF16)


def pool_kernel(returned, slots, pool, block_two, coarse, total):
    step = pl.program_id(0)
    slot = slots[1:2, :]
    high = (slot >> 5).astype(F32)
    low = (slot & 31).astype(F32)
    row = iota((8, PTS), 0)
    digits = jnp.where(row == 0, high, jnp.where(row == 1, low, 0.0)).astype(BF16)
    child = iota((128, PTS), 0)
    order = onehot(iota((128, PTS), 1) == POOL * (child & 63) + 2 * step + (child >> 6))
    found = mm_nt(order, digits)
    at = (found[:, 0:1] * 32.0 + found[:, 1:2]).astype(I32)
    pick = onehot(iota((128, SLOTS), 1) == at)
    two = mm(pick, returned[...]).astype(BF16)
    block_two[...] = two

    @pl.when(step == 0)
    def _():
        total[...] = jnp.zeros_like(total)

    for half in range(2):
        rows = slice(32 * half, 32 * half + 32)
        lanes = slice(512 * half, 512 * half + 512)
        weight = pool[:, 0, rows, :].reshape(512, 512)
        total[:, lanes] += mm(two[:CROWS], weight[:C]) + mm(two[CROWS:], weight[C:])

    @pl.when(step == N_HID - 1)
    def _():
        coarse[...] = total[...].astype(BF16)


def coarse_kernel(
    own,
    from_z,
    pair,
    pair_z,
    gains,
    heads,
    own_gate_up,
    own_down,
    far_gate_up,
    far_down,
    mid,
    kept,
    kept_z,
    sent,
    normed,
    total,
    out,
):
    step = pl.program_id(0)
    sources = (own, from_z, pair, pair_z)

    @pl.when(step == 0)
    def _():
        for at, ref in enumerate(sources):
            values = ref[...].astype(F32)
            normed[CROWS * at : CROWS * at + CROWS, :] = rms(values, gains[0:1, :])
            total[CROWS * at : CROWS * at + CROWS, :] = values

    @pl.when(step < N_HID)
    def _():
        def weight(which):
            rows = slice(16 * which, 16 * which + 16)
            return jnp.stack(
                [heads[:, 0, rows, 128 * part : 128 * part + 128] for part in range(4)], axis=1
            ).reshape(CC, 128)

        for ball in range(N_BALL):
            lanes = slice(128 * (ball % 8), 128 * (ball % 8) + 128)
            for part in range(4):
                top = 64 * (ball // 8) + 16 * part
                out[top : top + 16, lanes] = heads[ball, 0, 48:64, 128 * part : 128 * part + 128]

        rows = normed[...]
        q = mm(rows, weight(0)).astype(BF16)
        k = mm(rows, weight(1)).astype(BF16)
        v = mm(rows, weight(2)).astype(BF16)
        head_of = iota((BALL, 128), 1) // 64
        scale = LOG2E / math.sqrt(64)
        mixed = jnp.zeros((BALL, 128), F32)
        inverse = jnp.zeros((BALL, 128), F32)
        zero = jnp.zeros((BALL, 128), BF16)
        for head in range(2):
            mine = head_of == head
            scores = mm_nt(q, jnp.where(mine, k, zero))
            top = jnp.max(scores, axis=-1, keepdims=True)
            weights = jnp.exp2((scores - top) * scale)
            sums = jnp.sum(weights, axis=-1, keepdims=True)
            mixed = mixed + mm(weights.astype(BF16), jnp.where(mine, v, zero))
            inverse = jnp.where(mine, 1.0 / sums, inverse)
        total[...] += mm((mixed * inverse).astype(BF16), out[...])

    @pl.when(step == N_HID)
    def _():
        values = total[...].astype(BF16)
        mid[...] = values[:CROWS]
        normed[...] = rms(values.astype(F32), gains[1:2, :])
        total[...] = jnp.zeros_like(total)

    def mlp(gate_up, down):
        rows = normed[...]
        hidden = (silu(mm(rows, gate_up[0])) * mm(rows, gate_up[1])).astype(BF16)
        total[...] += mm(hidden, down[...])

    @pl.when((step >= N_HID) & (step < N_HID + 2))
    def _():
        mlp(own_gate_up, own_down)

    @pl.when(step >= N_HID + 2)
    def _():
        mlp(far_gate_up, far_down)

    @pl.when(step == N_HID + 3)
    def _():
        kept[...] = total[:CROWS, :]
        kept_z[...] = total[CROWS : 2 * CROWS, :]
        sent[...] = total[2 * CROWS :, :].astype(BF16)


def unpool_kernel(mid, kept, got, got_z, unpool, block_two, joined, done, children):
    step = pl.program_id(0)

    @pl.when(step == 0)
    def _():
        parts = kept[...] + got[...].astype(F32) + got_z[...].astype(F32)
        done[...] = (mid[...].astype(F32) + parts).astype(BF16)

    spread = mm(done[...], unpool[...].reshape(CC, 512)).astype(BF16).astype(F32)
    start = pl.multiple_of(step * 128, 128)
    two = block_two[...].astype(F32)
    children[pl.ds(start, CROWS), :] = (two[:CROWS] + spread[:, :C]).astype(BF16)
    children[pl.ds(start + CROWS, CROWS), :] = (two[CROWS:] + spread[:, C:]).astype(BF16)

    @pl.when(step == N_HID - 1)
    def _():
        for chunk in range(4):
            point = iota((256, PTS), 0) + chunk * 256
            child = iota((256, PTS), 1)
            order = onehot(point == POOL * (child & 63) + (child >> 6))
            joined[chunk * 256 : (chunk + 1) * 256, :] = mm(order, children[...]).astype(BF16)


def shape(dims, dtype):
    return jax.ShapeDtypeStruct(dims, dtype)


def whole(dims):
    zeros = (0,) * len(dims)
    return pl.BlockSpec(dims, lambda *_: zeros)


def layer(dims, which):
    index = (which,) + (0,) * (len(dims) - 1)
    return pl.BlockSpec((1,) + dims[1:], lambda *_: index)


def unit(which):
    return pl.BlockSpec(
        (N_BALL, 1, 64, 512), lambda i: (0, jnp.minimum(i, N_HID - 1), which, 0)
    )


def hidden_half(first, gate_up):
    if gate_up:
        return pl.BlockSpec((2, CC, 256), lambda i: (0, 0, jnp.clip(i - first, 0, 1)))
    return pl.BlockSpec((256, CC), lambda i: (jnp.clip(i - first, 0, 1), 0))


def exchange(values):
    return lax.all_to_all(values, ALL, split_axis=0, concat_axis=0, tiled=True)


def other_core(values):
    return lax.ppermute(values, "core", [(0, 1), (1, 0)])


def other_z(values):
    return lax.ppermute(values, "z", [(0, 1), (1, 0), (2, 3), (3, 2)])


def far_z(values):
    return lax.ppermute(values, "z", [(0, 2), (2, 0), (1, 3), (3, 1)])


def fine(which, rows, place, slots, norm, qkv, out, gate_up, down):
    return pl.pallas_call(
        functools.partial(fine_kernel, which),
        grid=(1,),
        out_shape=shape((SLOTS, C), BF16),
        in_specs=[
            whole((SLOTS, C)),
            pl.BlockSpec((SLOTS, N_DEV), lambda i: (0, 2)),
            whole((2, PTS)),
            layer(norm.shape, which),
            layer(qkv.shape, which),
            layer(out.shape, which),
            layer(gate_up.shape, which),
            layer(down.shape, which),
        ],
        out_specs=whole((SLOTS, C)),
        scratch_shapes=[pltpu.VMEM((8, SLOTS), I32), pltpu.VMEM((PTS, C), BF16)],
        compiler_params=params(),
        cost_estimate=pl.CostEstimate(flops=8 * 10**9, bytes_accessed=4 * 2**20, transcendentals=0),
        name=f"fine_block_{which}",
    )(rows, place, slots, norm, qkv, out, gate_up, down)


def body(
    points,
    tree_slot,
    rotated_slot,
    fine_norm,
    fine_qkv,
    fine_out,
    fine_gate_up,
    fine_down,
    pool_weight,
    coarse_norm,
    coarse_qkv,
    coarse_out,
    coarse_gate_up,
    coarse_down,
    unpool_weight,
):
    piece = pl.pallas_call(
        slice_kernel,
        grid_spec=pltpu.PrefetchScalarGridSpec(
            num_scalar_prefetch=1,
            grid=(1,),
            in_specs=[
                pl.BlockSpec((32, CC), lambda i, at: (at[0], 0)),
                pl.BlockSpec((64, 512), lambda i, at: (at[0], 0)),
                pl.BlockSpec((3, 64, 128), lambda i, at: (0, at[0], 0)),
                pl.BlockSpec((64, 128), lambda i, at: (at[0] // 8, at[0] % 8)),
            ],
            out_specs=pl.BlockSpec((192, 512), lambda i, at: (0, 0)),
        ),
        out_shape=shape((192, 512), BF16),
        compiler_params=params(),
        name="cut",
    )(
        lax.axis_index("ball").reshape(1),
        pool_weight,
        unpool_weight,
        coarse_qkv,
        coarse_out,
    )
    weights = lax.all_gather(piece, ALL).reshape(N_BALL, N_HID, 192, 512)
    far_gate_up = far_z(coarse_gate_up)
    far_down = far_z(coarse_down)

    send, slots = pl.pallas_call(
        prep_kernel,
        out_shape=(shape((SLOTS, C + N_DEV), BF16), shape((2, PTS), I32)),
        compiler_params=params(),
        name="prep",
    )(points, tree_slot.reshape(1, PTS), rotated_slot.reshape(1, PTS))
    first = exchange(send)
    fine_weights = (fine_norm, fine_qkv, fine_out, fine_gate_up, fine_down)
    rows = exchange(fine(0, first, first, slots, *fine_weights))
    returned = exchange(fine(1, rows, first, slots, *fine_weights))

    block_two, coarse = pl.pallas_call(
        pool_kernel,
        grid=(N_HID,),
        out_shape=(shape((PTS, C), BF16), shape((CROWS, CC), BF16)),
        in_specs=[whole((SLOTS, C)), whole((2, PTS)), unit(0)],
        out_specs=(pl.BlockSpec((128, C), lambda i: (i, 0)), whole((CROWS, CC))),
        scratch_shapes=[pltpu.VMEM((CROWS, CC), F32)],
        compiler_params=params(),
        name="pool",
    )(returned, slots, weights)

    from_z = other_z(coarse)
    rows_64 = whole((CROWS, CC))
    mid, kept, kept_z, sent = pl.pallas_call(
        coarse_kernel,
        grid=(N_HID + 4,),
        out_shape=(
            shape((CROWS, CC), BF16),
            shape((CROWS, CC), F32),
            shape((CROWS, CC), F32),
            shape((2 * CROWS, CC), BF16),
        ),
        in_specs=[
            rows_64,
            rows_64,
            rows_64,
            rows_64,
            whole((2, CC)),
            unit(2),
            hidden_half(N_HID, True),
            hidden_half(N_HID, False),
            hidden_half(N_HID + 2, True),
            hidden_half(N_HID + 2, False),
        ],
        out_specs=(rows_64, rows_64, rows_64, whole((2 * CROWS, CC))),
        scratch_shapes=[
            pltpu.VMEM((4 * CROWS, CC), BF16),
            pltpu.VMEM((4 * CROWS, CC), F32),
            pltpu.VMEM((128, CC), BF16),
        ],
        compiler_params=params(),
        name="coarse",
    )(
        coarse,
        from_z,
        other_core(coarse),
        other_core(from_z),
        coarse_norm,
        weights,
        coarse_gate_up,
        coarse_down,
        far_gate_up,
        far_down,
    )

    got = other_core(sent)
    got_z = other_z((kept_z + got[CROWS:].astype(F32)).astype(BF16))
    return pl.pallas_call(
        unpool_kernel,
        grid=(N_HID,),
        out_shape=shape((PTS, C), BF16),
        in_specs=[
            rows_64,
            rows_64,
            rows_64,
            rows_64,
            unit(1),
            pl.BlockSpec((128, C), lambda i: (i, 0)),
        ],
        out_specs=whole((PTS, C)),
        scratch_shapes=[pltpu.VMEM((CROWS, CC), BF16), pltpu.VMEM((PTS, C), BF16)],
        compiler_params=params(),
        name="unpool",
    )(mid, kept, got, got_z, weights, block_two)


def solution(mesh):
    split = Mesh(mesh.devices.reshape(N_BALL, N_Z, 2), ALL)
    hid = ("z", "core")
    placed = (
        P(ALL, None),
        P(ALL),
        P(ALL),
        P(),
        P(),
        P(),
        P(),
        P(),
        P(hid, None),
        P(),
        P(None, None, hid),
        P(hid, None),
        P(None, None, hid),
        P(hid, None),
        P(None, hid),
    )
    return jax.shard_map(
        body, mesh=split, in_specs=placed, out_specs=P(ALL, None), check_vma=False
    )
```

```python
import functools
import math

import jax
import jax.numpy as jnp
from jax import lax
from jax.experimental import pallas as pl
from jax.experimental.pallas import tpu as pltpu
from jax.sharding import Mesh
from jax.sharding import PartitionSpec as P

F32 = jnp.float32
BF16 = jnp.bfloat16
I32 = jnp.int32

C = 256
FH = 1024
FHEADS = 8
BALL = 256
POOL = 16
CC = 1024
N_DEV = 128
CAP = 16
PTS = 1024
SLOTS = N_DEV * CAP
CROWS = PTS // POOL
N_BALL = 16
N_Z = 4
N_HID = 8
EPS = 1e-06
LOG2E = 1.4426950408889634
ALL = ("ball", "z", "core")
VMEM_LIMIT = 56 * 2**20

NT = (((1,), (1,)), ((), ()))


def params():
    return pltpu.CompilerParams(vmem_limit_bytes=VMEM_LIMIT)


def iota(shape, dim):
    return lax.broadcasted_iota(I32, shape, dim)


def onehot(mask):
    return jnp.where(mask, 1.0, 0.0).astype(BF16)


def mm(a, b):
    return jnp.dot(a, b, preferred_element_type=F32)


def mm_nt(a, b):
    return lax.dot_general(a, b, NT, preferred_element_type=F32)


def rms(values, gain):
    mean_square = jnp.mean(values * values, axis=-1, keepdims=True)
    return (values * lax.rsqrt(mean_square + EPS) * gain).astype(BF16)


def silu(v):
    return 0.5 * v * (1.0 + jnp.tanh(0.5 * v))


def slice_kernel(at_ball, gate_up, down, pool, unpool, qkv, out, mlp, piece):
    mlp[0:64, :] = gate_up[0]
    mlp[64:128, :] = gate_up[1]
    mlp[128:160, :] = down[:, :512]
    mlp[160:192, :] = down[:, 512:]
    piece[0:32, :] = pool[:, :512]
    piece[32:64, :] = pool[:, 512:]
    piece[64:128, :] = unpool[...]
    for part in range(4):
        rows = slice(16 * part, 16 * part + 16)
        lanes = slice(128 * part, 128 * part + 128)
        for which in range(3):
            piece[128 + 16 * which : 144 + 16 * which, lanes] = qkv[which, rows, :]
        piece[176:192, lanes] = out[rows, :]


def prep_kernel(points, tree, rot, send, slots):
    upper = onehot(iota((PTS, PTS), 0) < iota((PTS, PTS), 1))
    device = iota((N_DEV, PTS), 0)
    digits = []
    for which, ref in ((0, tree), (1, rot)):
        target = ref[...]
        owner = target >> 10
        within = (target & (PTS - 1)) + 1
        match = jnp.where(device == owner, 1.0, 0.0)
        before = mm(match.astype(BF16), upper)
        rank = jnp.sum(match * before, axis=0, keepdims=True).astype(I32)
        slots[which : which + 1, :] = owner * CAP + rank
        row = device - 2 * which
        high = (within >> 5).astype(F32)
        low = (within & 31).astype(F32)
        digits.append(jnp.where(row == 0, high, jnp.where(row == 1, low, 0.0)).astype(BF16))
    for chunk in range(SLOTS // 256):
        rows = slice(chunk * 256, (chunk + 1) * 256)
        slot = iota((256, PTS), 0) + chunk * 256
        tree_pick = onehot(slot == slots[0:1, :])
        rot_pick = onehot(slot == slots[1:2, :])
        send[rows, :C] = mm(tree_pick, points[...]).astype(BF16)
        send[rows, C:] = (mm_nt(tree_pick, digits[0]) + mm_nt(rot_pick, digits[1])).astype(BF16)


def pack(slot_row, source, send):
    for chunk in range(SLOTS // 256):
        pick = onehot(iota((256, PTS), 0) + chunk * 256 == slot_row)
        send[chunk * 256 : (chunk + 1) * 256, :] = mm(pick, source[...]).astype(BF16)


def fine_ball(x_16, gains, qkv, out, gate_up, down):
    x = x_16.astype(F32)
    normed = rms(x, gains[0, 0:1, :])
    q = mm(normed, qkv[0, 0]).astype(BF16)
    k = mm(normed, qkv[0, 1]).astype(BF16)
    v = mm(normed, qkv[0, 2]).astype(BF16)
    width = C // FHEADS
    head_of = iota((BALL, C), 1) // width
    scale = LOG2E / math.sqrt(width)
    mixed = jnp.zeros((BALL, C), F32)
    inverse = jnp.zeros((BALL, C), F32)
    zero = jnp.zeros((BALL, C), BF16)
    for head in range(FHEADS):
        mine = head_of == head
        scores = mm_nt(q, jnp.where(mine, k, zero))
        top = jnp.max(scores, axis=-1, keepdims=True)
        weights = jnp.exp2((scores - top) * scale)
        total = jnp.sum(weights, axis=-1, keepdims=True)
        mixed = mixed + mm(weights.astype(BF16), jnp.where(mine, v, zero))
        inverse = jnp.where(mine, 1.0 / total, inverse)
    mixed = (mixed * inverse).astype(BF16)
    attended = (x + mm(mixed, out[0])).astype(BF16).astype(F32)
    normed = rms(attended, gains[0, 1:2, :])
    hidden = (silu(mm(normed, gate_up[0, 0])) * mm(normed, gate_up[0, 1])).astype(BF16)
    return (attended + mm(hidden, down[0])).astype(BF16)


def fine_kernel(which, rows, place, slots, gains, qkv, out, gate_up, down, send, place_row, states):
    row = iota((8, N_DEV), 0)
    lane = iota((8, N_DEV), 1)
    digit = jnp.where(row == 0, jnp.where(lane == 2 * which, 32.0, 0.0), 0.0)
    digit = jnp.where((row == 0) & (lane == 2 * which + 1), 1.0, digit).astype(BF16)
    place_row[...] = mm_nt(digit, place[...]).astype(I32) - 1

    def one_ball(ball, carry):
        start = pl.multiple_of(ball * BALL, BALL)
        pick = onehot(iota((BALL, SLOTS), 0) + ball * BALL == place_row[0:1, :])
        x = mm(pick, rows[...]).astype(BF16)
        states[pl.ds(start, BALL), :] = fine_ball(x, gains, qkv, out, gate_up, down)
        return carry

    lax.fori_loop(0, PTS // BALL, one_ball, 0)

    if which == 0:
        pack(slots[1:2, :], states, send)
        return
    for chunk in range(SLOTS // 256):
        digits = place[chunk * 256 : (chunk + 1) * 256, :].astype(F32)
        at = (digits[:, 2:3] * 32.0 + digits[:, 3:4]).astype(I32) - 1
        pick = onehot(iota((256, PTS), 1) == at)
        send[chunk * 256 : (chunk + 1) * 256, :] = mm(pick, states[...]).astype(BF16)


def pool_kernel(returned, slots, pool, block_two, coarse, total):
    step = pl.program_id(0)
    slot = slots[1:2, :]
    high = (slot >> 5).astype(F32)
    low = (slot & 31).astype(F32)
    row = iota((8, PTS), 0)
    digits = jnp.where(row == 0, high, jnp.where(row == 1, low, 0.0)).astype(BF16)
    child = iota((128, PTS), 0)
    order = onehot(iota((128, PTS), 1) == POOL * (child & 63) + 2 * step + (child >> 6))
    found = mm_nt(order, digits)
    at = (found[:, 0:1] * 32.0 + found[:, 1:2]).astype(I32)
    pick = onehot(iota((128, SLOTS), 1) == at)
    two = mm(pick, returned[...]).astype(BF16)
    block_two[...] = two

    @pl.when(step == 0)
    def _():
        total[...] = jnp.zeros_like(total)

    for half in range(2):
        rows = slice(32 * half, 32 * half + 32)
        lanes = slice(512 * half, 512 * half + 512)
        weight = pool[:, 0, rows, :].reshape(512, 512)
        total[:, lanes] += mm(two[:CROWS], weight[:C]) + mm(two[CROWS:], weight[C:])

    @pl.when(step == N_HID - 1)
    def _():
        coarse[...] = total[...].astype(BF16)


def coarse_kernel(
    own,
    from_z,
    pair,
    pair_z,
    gains,
    heads,
    own_gate_up,
    own_down,
    far_gate,
    far_up,
    far_down,
    mid,
    kept,
    kept_z,
    sent,
    normed,
    total,
    out,
):
    step = pl.program_id(0)
    sources = (own, from_z, pair, pair_z)

    @pl.when(step == 0)
    def _():
        for at, ref in enumerate(sources):
            values = ref[...].astype(F32)
            normed[CROWS * at : CROWS * at + CROWS, :] = rms(values, gains[0:1, :])
            total[CROWS * at : CROWS * at + CROWS, :] = values

    @pl.when(step < N_HID)
    def _():
        def weight(which):
            rows = slice(16 * which, 16 * which + 16)
            return jnp.stack(
                [heads[:, 0, rows, 128 * part : 128 * part + 128] for part in range(4)], axis=1
            ).reshape(CC, 128)

        for ball in range(N_BALL):
            lanes = slice(128 * (ball % 8), 128 * (ball % 8) + 128)
            for part in range(4):
                top = 64 * (ball // 8) + 16 * part
                out[top : top + 16, lanes] = heads[ball, 0, 48:64, 128 * part : 128 * part + 128]

        rows = normed[...]
        q = mm(rows, weight(0)).astype(BF16)
        k = mm(rows, weight(1)).astype(BF16)
        v = mm(rows, weight(2)).astype(BF16)
        head_of = iota((BALL, 128), 1) // 64
        scale = LOG2E / math.sqrt(64)
        mixed = jnp.zeros((BALL, 128), F32)
        inverse = jnp.zeros((BALL, 128), F32)
        zero = jnp.zeros((BALL, 128), BF16)
        for head in range(2):
            mine = head_of == head
            scores = mm_nt(q, jnp.where(mine, k, zero))
            top = jnp.max(scores, axis=-1, keepdims=True)
            weights = jnp.exp2((scores - top) * scale)
            sums = jnp.sum(weights, axis=-1, keepdims=True)
            mixed = mixed + mm(weights.astype(BF16), jnp.where(mine, v, zero))
            inverse = jnp.where(mine, 1.0 / sums, inverse)
        total[...] += mm((mixed * inverse).astype(BF16), out[...])

    @pl.when(step == N_HID)
    def _():
        values = total[...].astype(BF16)
        mid[...] = values[:CROWS]
        normed[...] = rms(values.astype(F32), gains[1:2, :])
        total[...] = jnp.zeros_like(total)

    def hidden_of(gate, up):
        rows = normed[...]
        return (silu(mm(rows, gate)) * mm(rows, up)).astype(BF16)

    @pl.when((step >= N_HID) & (step < N_HID + 2))
    def _():
        total[...] += mm(hidden_of(own_gate_up[0], own_gate_up[1]), own_down[...])

    @pl.when(step >= N_HID + 2)
    def _():
        hidden = hidden_of(far_gate[...].reshape(CC, 256), far_up[...].reshape(CC, 256))
        total[:, :512] += mm(hidden, far_down[:, :32, :].reshape(256, 512))
        total[:, 512:] += mm(hidden, far_down[:, 32:, :].reshape(256, 512))

    @pl.when(step == N_HID + 3)
    def _():
        kept[...] = total[:CROWS, :]
        kept_z[...] = total[CROWS : 2 * CROWS, :]
        sent[...] = total[2 * CROWS :, :].astype(BF16)


def unpool_kernel(mid, kept, got, got_z, unpool, block_two, joined, done, children):
    step = pl.program_id(0)

    @pl.when(step == 0)
    def _():
        parts = kept[...] + got[...].astype(F32) + got_z[...].astype(F32)
        done[...] = (mid[...].astype(F32) + parts).astype(BF16)

    spread = mm(done[...], unpool[...].reshape(CC, 512)).astype(BF16).astype(F32)
    start = pl.multiple_of(step * 128, 128)
    two = block_two[...].astype(F32)
    children[pl.ds(start, CROWS), :] = (two[:CROWS] + spread[:, :C]).astype(BF16)
    children[pl.ds(start + CROWS, CROWS), :] = (two[CROWS:] + spread[:, C:]).astype(BF16)

    @pl.when(step == N_HID - 1)
    def _():
        for chunk in range(4):
            point = iota((256, PTS), 0) + chunk * 256
            child = iota((256, PTS), 1)
            order = onehot(point == POOL * (child & 63) + (child >> 6))
            joined[chunk * 256 : (chunk + 1) * 256, :] = mm(order, children[...]).astype(BF16)


def shape(dims, dtype):
    return jax.ShapeDtypeStruct(dims, dtype)


def whole(dims):
    zeros = (0,) * len(dims)
    return pl.BlockSpec(dims, lambda *_: zeros)


def layer(dims, which):
    index = (which,) + (0,) * (len(dims) - 1)
    return pl.BlockSpec((1,) + dims[1:], lambda *_: index)


def unit(which):
    return pl.BlockSpec(
        (N_BALL, 1, 64, 512), lambda i: (0, jnp.minimum(i, N_HID - 1), which, 0)
    )


def hidden_half(first, gate_up):
    if gate_up:
        return pl.BlockSpec((2, CC, 256), lambda i: (0, 0, jnp.clip(i - first, 0, 1)))
    return pl.BlockSpec((256, CC), lambda i: (jnp.clip(i - first, 0, 1), 0))


def far_halves(first):
    def half(i):
        return jnp.clip(i - first, 0, 1)

    return (
        pl.BlockSpec((N_BALL, 64, 256), lambda i: (0, 0, half(i))),
        pl.BlockSpec((N_BALL, 64, 256), lambda i: (0, 1, half(i))),
        pl.BlockSpec((N_BALL // 2, 64, 512), lambda i: (half(i), 2, 0)),
    )


def exchange(values):
    return lax.all_to_all(values, ALL, split_axis=0, concat_axis=0, tiled=True)


def other_core(values):
    return lax.ppermute(values, "core", [(0, 1), (1, 0)])


def other_z(values):
    return lax.ppermute(values, "z", [(0, 1), (1, 0), (2, 3), (3, 2)])


def far_z(values):
    return lax.ppermute(values, "z", [(0, 2), (2, 0), (1, 3), (3, 1)])


def fine(which, rows, place, slots, norm, qkv, out, gate_up, down):
    return pl.pallas_call(
        functools.partial(fine_kernel, which),
        grid=(1,),
        out_shape=shape((SLOTS, C), BF16),
        in_specs=[
            whole((SLOTS, C)),
            pl.BlockSpec((SLOTS, N_DEV), lambda i: (0, 2)),
            whole((2, PTS)),
            layer(norm.shape, which),
            layer(qkv.shape, which),
            layer(out.shape, which),
            layer(gate_up.shape, which),
            layer(down.shape, which),
        ],
        out_specs=whole((SLOTS, C)),
        scratch_shapes=[pltpu.VMEM((8, SLOTS), I32), pltpu.VMEM((PTS, C), BF16)],
        compiler_params=params(),
        cost_estimate=pl.CostEstimate(flops=8 * 10**9, bytes_accessed=4 * 2**20, transcendentals=0),
        name=f"fine_block_{which}",
    )(rows, place, slots, norm, qkv, out, gate_up, down)


def body(
    points,
    tree_slot,
    rotated_slot,
    fine_norm,
    fine_qkv,
    fine_out,
    fine_gate_up,
    fine_down,
    pool_weight,
    coarse_norm,
    coarse_qkv,
    coarse_out,
    coarse_gate_up,
    coarse_down,
    unpool_weight,
):
    mlp_piece, piece = pl.pallas_call(
        slice_kernel,
        grid_spec=pltpu.PrefetchScalarGridSpec(
            num_scalar_prefetch=1,
            grid=(1,),
            in_specs=[
                pl.BlockSpec((2, 64, 512), lambda i, at: (0, at[0], 0)),
                pl.BlockSpec((32, CC), lambda i, at: (at[0], 0)),
                pl.BlockSpec((32, CC), lambda i, at: (at[0], 0)),
                pl.BlockSpec((64, 512), lambda i, at: (at[0], 0)),
                pl.BlockSpec((3, 64, 128), lambda i, at: (0, at[0], 0)),
                pl.BlockSpec((64, 128), lambda i, at: (at[0] // 8, at[0] % 8)),
            ],
            out_specs=(pl.BlockSpec((192, 512), lambda i, at: (0, 0)),) * 2,
        ),
        out_shape=(shape((192, 512), BF16),) * 2,
        compiler_params=params(),
        name="cut",
    )(
        lax.axis_index("ball").reshape(1),
        coarse_gate_up,
        coarse_down,
        pool_weight,
        unpool_weight,
        coarse_qkv,
        coarse_out,
    )
    weights = lax.all_gather(piece, ALL).reshape(N_BALL, N_HID, 192, 512)

    send, slots = pl.pallas_call(
        prep_kernel,
        out_shape=(shape((SLOTS, C + N_DEV), BF16), shape((2, PTS), I32)),
        compiler_params=params(),
        cost_estimate=pl.CostEstimate(flops=6 * 10**9, bytes_accessed=2 * 2**20, transcendentals=0),
        name="prep",
    )(points, tree_slot.reshape(1, PTS), rotated_slot.reshape(1, PTS))
    far_piece, send = lax.optimization_barrier((far_z(mlp_piece), send))
    far_mlp = lax.all_gather(far_piece, "ball")
    first = exchange(send)
    fine_weights = (fine_norm, fine_qkv, fine_out, fine_gate_up, fine_down)
    rows = exchange(fine(0, first, first, slots, *fine_weights))
    returned = exchange(fine(1, rows, first, slots, *fine_weights))

    block_two, coarse = pl.pallas_call(
        pool_kernel,
        grid=(N_HID,),
        out_shape=(shape((PTS, C), BF16), shape((CROWS, CC), BF16)),
        in_specs=[whole((SLOTS, C)), whole((2, PTS)), unit(0)],
        out_specs=(pl.BlockSpec((128, C), lambda i: (i, 0)), whole((CROWS, CC))),
        scratch_shapes=[pltpu.VMEM((CROWS, CC), F32)],
        compiler_params=params(),
        name="pool",
    )(returned, slots, weights)

    from_z = other_z(coarse)
    rows_64 = whole((CROWS, CC))
    mid, kept, kept_z, sent = pl.pallas_call(
        coarse_kernel,
        grid=(N_HID + 4,),
        out_shape=(
            shape((CROWS, CC), BF16),
            shape((CROWS, CC), F32),
            shape((CROWS, CC), F32),
            shape((2 * CROWS, CC), BF16),
        ),
        in_specs=[
            rows_64,
            rows_64,
            rows_64,
            rows_64,
            whole((2, CC)),
            unit(2),
            hidden_half(N_HID, True),
            hidden_half(N_HID, False),
            *far_halves(N_HID + 2),
        ],
        out_specs=(rows_64, rows_64, rows_64, whole((2 * CROWS, CC))),
        scratch_shapes=[
            pltpu.VMEM((4 * CROWS, CC), BF16),
            pltpu.VMEM((4 * CROWS, CC), F32),
            pltpu.VMEM((128, CC), BF16),
        ],
        compiler_params=params(),
        name="coarse",
    )(
        coarse,
        from_z,
        other_core(coarse),
        other_core(from_z),
        coarse_norm,
        weights,
        coarse_gate_up,
        coarse_down,
        far_mlp,
        far_mlp,
        far_mlp,
    )

    got = other_core(sent)
    got_z = other_z((kept_z + got[CROWS:].astype(F32)).astype(BF16))
    return pl.pallas_call(
        unpool_kernel,
        grid=(N_HID,),
        out_shape=shape((PTS, C), BF16),
        in_specs=[
            rows_64,
            rows_64,
            rows_64,
            rows_64,
            unit(1),
            pl.BlockSpec((128, C), lambda i: (i, 0)),
        ],
        out_specs=whole((PTS, C)),
        scratch_shapes=[pltpu.VMEM((CROWS, CC), BF16), pltpu.VMEM((PTS, C), BF16)],
        compiler_params=params(),
        name="unpool",
    )(mid, kept, got, got_z, weights, block_two)


def solution(mesh):
    split = Mesh(mesh.devices.reshape(N_BALL, N_Z, 2), ALL)
    hid = ("z", "core")
    placed = (
        P(ALL, None),
        P(ALL),
        P(ALL),
        P(),
        P(),
        P(),
        P(),
        P(),
        P(hid, None),
        P(),
        P(None, None, hid),
        P(hid, None),
        P(None, None, hid),
        P(hid, None),
        P(None, hid),
    )
    return jax.shard_map(
        body, mesh=split, in_specs=placed, out_specs=P(ALL, None), check_vma=False
    )
```

```python
import functools
import math

import jax
import jax.numpy as jnp
from jax import lax
from jax.experimental import pallas as pl
from jax.experimental.pallas import tpu as pltpu
from jax.sharding import Mesh
from jax.sharding import PartitionSpec as P

F32 = jnp.float32
BF16 = jnp.bfloat16
I32 = jnp.int32

C = 256
FH = 1024
FHEADS = 8
BALL = 256
POOL = 16
CC = 1024
N_DEV = 128
CAP = 16
PTS = 1024
SLOTS = N_DEV * CAP
CROWS = PTS // POOL
N_BALL = 16
N_Z = 4
N_HID = 8
EPS = 1e-06
LOG2E = 1.4426950408889634
ALL = ("ball", "z", "core")
VMEM_LIMIT = 56 * 2**20

NT = (((1,), (1,)), ((), ()))


def params():
    return pltpu.CompilerParams(vmem_limit_bytes=VMEM_LIMIT)


def iota(shape, dim):
    return lax.broadcasted_iota(I32, shape, dim)


def onehot(mask):
    return jnp.where(mask, 1.0, 0.0).astype(BF16)


def mm(a, b):
    return jnp.dot(a, b, preferred_element_type=F32)


def mm_nt(a, b):
    return lax.dot_general(a, b, NT, preferred_element_type=F32)


def rms(values, gain):
    mean_square = jnp.mean(values * values, axis=-1, keepdims=True)
    return (values * lax.rsqrt(mean_square + EPS) * gain).astype(BF16)


def silu(v):
    return 0.5 * v * (1.0 + jnp.tanh(0.5 * v))


def slice_kernel(at_ball, pool, unpool, qkv, out, piece):
    piece[0:32, :] = pool[:, :512]
    piece[32:64, :] = pool[:, 512:]
    piece[64:128, :] = unpool[...]
    for part in range(4):
        rows = slice(16 * part, 16 * part + 16)
        lanes = slice(128 * part, 128 * part + 128)
        for which in range(3):
            piece[128 + 16 * which : 144 + 16 * which, lanes] = qkv[which, rows, :]
        piece[176:192, lanes] = out[rows, :]


def prep_kernel(points, tree, rot, send, slots):
    upper = onehot(iota((PTS, PTS), 0) < iota((PTS, PTS), 1))
    device = iota((N_DEV, PTS), 0)
    digits = []
    for which, ref in ((0, tree), (1, rot)):
        target = ref[...]
        owner = target >> 10
        within = (target & (PTS - 1)) + 1
        match = jnp.where(device == owner, 1.0, 0.0)
        before = mm(match.astype(BF16), upper)
        rank = jnp.sum(match * before, axis=0, keepdims=True).astype(I32)
        slots[which : which + 1, :] = owner * CAP + rank
        row = device - 2 * which
        high = (within >> 5).astype(F32)
        low = (within & 31).astype(F32)
        digits.append(jnp.where(row == 0, high, jnp.where(row == 1, low, 0.0)).astype(BF16))
    for chunk in range(SLOTS // 256):
        rows = slice(chunk * 256, (chunk + 1) * 256)
        slot = iota((256, PTS), 0) + chunk * 256
        tree_pick = onehot(slot == slots[0:1, :])
        rot_pick = onehot(slot == slots[1:2, :])
        send[rows, :C] = mm(tree_pick, points[...]).astype(BF16)
        send[rows, C:] = (mm_nt(tree_pick, digits[0]) + mm_nt(rot_pick, digits[1])).astype(BF16)


def pack(slot_row, source, send):
    for chunk in range(SLOTS // 256):
        pick = onehot(iota((256, PTS), 0) + chunk * 256 == slot_row)
        send[chunk * 256 : (chunk + 1) * 256, :] = mm(pick, source[...]).astype(BF16)


def fine_ball(x_16, gains, qkv, out, gate_up, down):
    x = x_16.astype(F32)
    normed = rms(x, gains[0, 0:1, :])
    q = mm(normed, qkv[0, 0]).astype(BF16)
    k = mm(normed, qkv[0, 1]).astype(BF16)
    v = mm(normed, qkv[0, 2]).astype(BF16)
    width = C // FHEADS
    head_of = iota((BALL, C), 1) // width
    scale = LOG2E / math.sqrt(width)
    mixed = jnp.zeros((BALL, C), F32)
    inverse = jnp.zeros((BALL, C), F32)
    zero = jnp.zeros((BALL, C), BF16)
    for head in range(FHEADS):
        mine = head_of == head
        scores = mm_nt(q, jnp.where(mine, k, zero))
        top = jnp.max(scores, axis=-1, keepdims=True)
        weights = jnp.exp2((scores - top) * scale)
        total = jnp.sum(weights, axis=-1, keepdims=True)
        mixed = mixed + mm(weights.astype(BF16), jnp.where(mine, v, zero))
        inverse = jnp.where(mine, 1.0 / total, inverse)
    mixed = (mixed * inverse).astype(BF16)
    attended = (x + mm(mixed, out[0])).astype(BF16).astype(F32)
    normed = rms(attended, gains[0, 1:2, :])
    hidden = (silu(mm(normed, gate_up[0, 0])) * mm(normed, gate_up[0, 1])).astype(BF16)
    return (attended + mm(hidden, down[0])).astype(BF16)


def fine_kernel(which, rows, place, slots, gains, qkv, out, gate_up, down, send, place_row, states):
    row = iota((8, N_DEV), 0)
    lane = iota((8, N_DEV), 1)
    digit = jnp.where(row == 0, jnp.where(lane == 2 * which, 32.0, 0.0), 0.0)
    digit = jnp.where((row == 0) & (lane == 2 * which + 1), 1.0, digit).astype(BF16)
    place_row[...] = mm_nt(digit, place[...]).astype(I32) - 1

    def one_ball(ball, carry):
        start = pl.multiple_of(ball * BALL, BALL)
        pick = onehot(iota((BALL, SLOTS), 0) + ball * BALL == place_row[0:1, :])
        x = mm(pick, rows[...]).astype(BF16)
        states[pl.ds(start, BALL), :] = fine_ball(x, gains, qkv, out, gate_up, down)
        return carry

    lax.fori_loop(0, PTS // BALL, one_ball, 0)

    if which == 0:
        pack(slots[1:2, :], states, send)
        return
    for chunk in range(SLOTS // 256):
        digits = place[chunk * 256 : (chunk + 1) * 256, :].astype(F32)
        at = (digits[:, 2:3] * 32.0 + digits[:, 3:4]).astype(I32) - 1
        pick = onehot(iota((256, PTS), 1) == at)
        send[chunk * 256 : (chunk + 1) * 256, :] = mm(pick, states[...]).astype(BF16)


def pool_kernel(returned, slots, pool, block_two, coarse, total):
    step = pl.program_id(0)
    slot = slots[1:2, :]
    high = (slot >> 5).astype(F32)
    low = (slot & 31).astype(F32)
    row = iota((8, PTS), 0)
    digits = jnp.where(row == 0, high, jnp.where(row == 1, low, 0.0)).astype(BF16)
    child = iota((128, PTS), 0)
    order = onehot(iota((128, PTS), 1) == POOL * (child & 63) + 2 * step + (child >> 6))
    found = mm_nt(order, digits)
    at = (found[:, 0:1] * 32.0 + found[:, 1:2]).astype(I32)
    pick = onehot(iota((128, SLOTS), 1) == at)
    two = mm(pick, returned[...]).astype(BF16)
    block_two[...] = two

    @pl.when(step == 0)
    def _():
        total[...] = jnp.zeros_like(total)

    for half in range(2):
        rows = slice(32 * half, 32 * half + 32)
        lanes = slice(512 * half, 512 * half + 512)
        weight = pool[:, 0, rows, :].reshape(512, 512)
        total[:, lanes] += mm(two[:CROWS], weight[:C]) + mm(two[CROWS:], weight[C:])

    @pl.when(step == N_HID - 1)
    def _():
        coarse[...] = total[...].astype(BF16)


def coarse_kernel(
    own,
    from_z,
    pair,
    pair_z,
    gains,
    heads,
    own_gate_up,
    own_down,
    far_gate,
    far_up,
    far_down,
    mid,
    kept,
    kept_z,
    sent,
    normed,
    total,
    out,
):
    step = pl.program_id(0)
    sources = (own, from_z, pair, pair_z)

    @pl.when(step == 0)
    def _():
        for at, ref in enumerate(sources):
            values = ref[...].astype(F32)
            normed[CROWS * at : CROWS * at + CROWS, :] = rms(values, gains[0:1, :])
            total[CROWS * at : CROWS * at + CROWS, :] = values

    @pl.when(step < N_HID)
    def _():
        def weight(which):
            rows = slice(16 * which, 16 * which + 16)
            return jnp.stack(
                [heads[:, 0, rows, 128 * part : 128 * part + 128] for part in range(4)], axis=1
            ).reshape(CC, 128)

        for ball in range(N_BALL):
            lanes = slice(128 * (ball % 8), 128 * (ball % 8) + 128)
            for part in range(4):
                top = 64 * (ball // 8) + 16 * part
                out[top : top + 16, lanes] = heads[ball, 0, 48:64, 128 * part : 128 * part + 128]

        rows = normed[...]
        q = mm(rows, weight(0)).astype(BF16)
        k = mm(rows, weight(1)).astype(BF16)
        v = mm(rows, weight(2)).astype(BF16)
        head_of = iota((BALL, 128), 1) // 64
        scale = LOG2E / math.sqrt(64)
        mixed = jnp.zeros((BALL, 128), F32)
        inverse = jnp.zeros((BALL, 128), F32)
        zero = jnp.zeros((BALL, 128), BF16)
        for head in range(2):
            mine = head_of == head
            scores = mm_nt(q, jnp.where(mine, k, zero))
            top = jnp.max(scores, axis=-1, keepdims=True)
            weights = jnp.exp2((scores - top) * scale)
            sums = jnp.sum(weights, axis=-1, keepdims=True)
            mixed = mixed + mm(weights.astype(BF16), jnp.where(mine, v, zero))
            inverse = jnp.where(mine, 1.0 / sums, inverse)
        total[...] += mm((mixed * inverse).astype(BF16), out[...])

    @pl.when(step == N_HID)
    def _():
        values = total[...].astype(BF16)
        mid[...] = values[:CROWS]
        normed[...] = rms(values.astype(F32), gains[1:2, :])
        total[...] = jnp.zeros_like(total)

    def hidden_of(gate, up):
        rows = normed[...]
        return (silu(mm(rows, gate)) * mm(rows, up)).astype(BF16)

    @pl.when((step >= N_HID) & (step < N_HID + 2))
    def _():
        total[...] += mm(hidden_of(own_gate_up[0], own_gate_up[1]), own_down[...])

    @pl.when(step >= N_HID + 2)
    def _():
        total[...] += mm(hidden_of(far_gate[...], far_up[...]), far_down[...])

    @pl.when(step == N_HID + 3)
    def _():
        kept[...] = total[:CROWS, :]
        kept_z[...] = total[CROWS : 2 * CROWS, :]
        sent[...] = total[2 * CROWS :, :].astype(BF16)


def unpool_kernel(mid, kept, got, got_z, unpool, block_two, joined, done, children):
    step = pl.program_id(0)

    @pl.when(step == 0)
    def _():
        parts = kept[...] + got[...].astype(F32) + got_z[...].astype(F32)
        done[...] = (mid[...].astype(F32) + parts).astype(BF16)

    spread = mm(done[...], unpool[...].reshape(CC, 512)).astype(BF16).astype(F32)
    start = pl.multiple_of(step * 128, 128)
    two = block_two[...].astype(F32)
    children[pl.ds(start, CROWS), :] = (two[:CROWS] + spread[:, :C]).astype(BF16)
    children[pl.ds(start + CROWS, CROWS), :] = (two[CROWS:] + spread[:, C:]).astype(BF16)

    @pl.when(step == N_HID - 1)
    def _():
        for chunk in range(4):
            point = iota((256, PTS), 0) + chunk * 256
            child = iota((256, PTS), 1)
            order = onehot(point == POOL * (child & 63) + (child >> 6))
            joined[chunk * 256 : (chunk + 1) * 256, :] = mm(order, children[...]).astype(BF16)


def shape(dims, dtype):
    return jax.ShapeDtypeStruct(dims, dtype)


def whole(dims):
    zeros = (0,) * len(dims)
    return pl.BlockSpec(dims, lambda *_: zeros)


def layer(dims, which):
    index = (which,) + (0,) * (len(dims) - 1)
    return pl.BlockSpec((1,) + dims[1:], lambda *_: index)


def unit(which):
    return pl.BlockSpec(
        (N_BALL, 1, 64, 512), lambda i: (0, jnp.minimum(i, N_HID - 1), which, 0)
    )


def hidden_half(first, kind):
    def half(i):
        return jnp.clip(i - first, 0, 1)

    if kind == "both":
        return pl.BlockSpec((2, CC, 256), lambda i: (0, 0, half(i)))
    if kind == "in":
        return pl.BlockSpec((CC, 256), lambda i: (0, half(i)))
    return pl.BlockSpec((256, CC), lambda i: (half(i), 0))


def exchange(values):
    return lax.all_to_all(values, ALL, split_axis=0, concat_axis=0, tiled=True)


def other_core(values):
    return lax.ppermute(values, "core", [(0, 1), (1, 0)])


def other_z(values):
    return lax.ppermute(values, "z", [(0, 1), (1, 0), (2, 3), (3, 2)])


def far_z(values):
    return lax.ppermute(values, "z", [(0, 3), (3, 0), (1, 2), (2, 1)])


def fine(which, rows, place, slots, norm, qkv, out, gate_up, down):
    return pl.pallas_call(
        functools.partial(fine_kernel, which),
        grid=(1,),
        out_shape=shape((SLOTS, C), BF16),
        in_specs=[
            whole((SLOTS, C)),
            pl.BlockSpec((SLOTS, N_DEV), lambda i: (0, 2)),
            whole((2, PTS)),
            layer(norm.shape, which),
            layer(qkv.shape, which),
            layer(out.shape, which),
            layer(gate_up.shape, which),
            layer(down.shape, which),
        ],
        out_specs=whole((SLOTS, C)),
        scratch_shapes=[pltpu.VMEM((8, SLOTS), I32), pltpu.VMEM((PTS, C), BF16)],
        compiler_params=params(),
        cost_estimate=pl.CostEstimate(flops=8 * 10**9, bytes_accessed=4 * 2**20, transcendentals=0),
        name=f"fine_block_{which}",
    )(rows, place, slots, norm, qkv, out, gate_up, down)


def body(
    points,
    tree_slot,
    rotated_slot,
    fine_norm,
    fine_qkv,
    fine_out,
    fine_gate_up,
    fine_down,
    pool_weight,
    coarse_norm,
    coarse_qkv,
    coarse_out,
    coarse_gate_up,
    coarse_down,
    unpool_weight,
):
    piece = pl.pallas_call(
        slice_kernel,
        grid_spec=pltpu.PrefetchScalarGridSpec(
            num_scalar_prefetch=1,
            grid=(1,),
            in_specs=[
                pl.BlockSpec((32, CC), lambda i, at: (at[0], 0)),
                pl.BlockSpec((64, 512), lambda i, at: (at[0], 0)),
                pl.BlockSpec((3, 64, 128), lambda i, at: (0, at[0], 0)),
                pl.BlockSpec((64, 128), lambda i, at: (at[0] // 8, at[0] % 8)),
            ],
            out_specs=pl.BlockSpec((192, 512), lambda i, at: (0, 0)),
        ),
        out_shape=shape((192, 512), BF16),
        compiler_params=params(),
        name="cut",
    )(
        lax.axis_index("ball").reshape(1),
        pool_weight,
        unpool_weight,
        coarse_qkv,
        coarse_out,
    )
    weights = lax.all_gather(piece, ALL).reshape(N_BALL, N_HID, 192, 512)

    send, slots = pl.pallas_call(
        prep_kernel,
        out_shape=(shape((SLOTS, C + N_DEV), BF16), shape((2, PTS), I32)),
        compiler_params=params(),
        cost_estimate=pl.CostEstimate(flops=6 * 10**9, bytes_accessed=2 * 2**20, transcendentals=0),
        name="prep",
    )(points, tree_slot.reshape(1, PTS), rotated_slot.reshape(1, PTS))
    first = exchange(send)
    far_gate, first = lax.optimization_barrier((far_z(coarse_gate_up[0]), first))
    fine_weights = (fine_norm, fine_qkv, fine_out, fine_gate_up, fine_down)
    rows = exchange(fine(0, first, first, slots, *fine_weights))
    far_up, rows = lax.optimization_barrier((far_z(coarse_gate_up[1]), rows))
    returned = exchange(fine(1, rows, first, slots, *fine_weights))
    far_down, returned = lax.optimization_barrier((far_z(coarse_down), returned))

    block_two, coarse = pl.pallas_call(
        pool_kernel,
        grid=(N_HID,),
        out_shape=(shape((PTS, C), BF16), shape((CROWS, CC), BF16)),
        in_specs=[whole((SLOTS, C)), whole((2, PTS)), unit(0)],
        out_specs=(pl.BlockSpec((128, C), lambda i: (i, 0)), whole((CROWS, CC))),
        scratch_shapes=[pltpu.VMEM((CROWS, CC), F32)],
        compiler_params=params(),
        name="pool",
    )(returned, slots, weights)

    from_z = other_z(coarse)
    rows_64 = whole((CROWS, CC))
    mid, kept, kept_z, sent = pl.pallas_call(
        coarse_kernel,
        grid=(N_HID + 4,),
        out_shape=(
            shape((CROWS, CC), BF16),
            shape((CROWS, CC), F32),
            shape((CROWS, CC), F32),
            shape((2 * CROWS, CC), BF16),
        ),
        in_specs=[
            rows_64,
            rows_64,
            rows_64,
            rows_64,
            whole((2, CC)),
            unit(2),
            hidden_half(N_HID, "both"),
            hidden_half(N_HID, "out"),
            hidden_half(N_HID + 2, "in"),
            hidden_half(N_HID + 2, "in"),
            hidden_half(N_HID + 2, "out"),
        ],
        out_specs=(rows_64, rows_64, rows_64, whole((2 * CROWS, CC))),
        scratch_shapes=[
            pltpu.VMEM((4 * CROWS, CC), BF16),
            pltpu.VMEM((4 * CROWS, CC), F32),
            pltpu.VMEM((128, CC), BF16),
        ],
        compiler_params=params(),
        name="coarse",
    )(
        coarse,
        from_z,
        other_core(coarse),
        other_core(from_z),
        coarse_norm,
        weights,
        coarse_gate_up,
        coarse_down,
        far_gate,
        far_up,
        far_down,
    )

    got = other_core(sent)
    got_z = other_z((kept_z + got[CROWS:].astype(F32)).astype(BF16))
    return pl.pallas_call(
        unpool_kernel,
        grid=(N_HID,),
        out_shape=shape((PTS, C), BF16),
        in_specs=[
            rows_64,
            rows_64,
            rows_64,
            rows_64,
            unit(1),
            pl.BlockSpec((128, C), lambda i: (i, 0)),
        ],
        out_specs=whole((PTS, C)),
        scratch_shapes=[pltpu.VMEM((CROWS, CC), BF16), pltpu.VMEM((PTS, C), BF16)],
        compiler_params=params(),
        name="unpool",
    )(mid, kept, got, got_z, weights, block_two)


def solution(mesh):
    split = Mesh(mesh.devices.reshape(N_BALL, N_Z, 2), ALL)
    hid = ("z", "core")
    placed = (
        P(ALL, None),
        P(ALL),
        P(ALL),
        P(),
        P(),
        P(),
        P(),
        P(),
        P(hid, None),
        P(),
        P(None, None, hid),
        P(hid, None),
        P(None, None, hid),
        P(hid, None),
        P(None, hid),
    )
    return jax.shard_map(
        body, mesh=split, in_specs=placed, out_specs=P(ALL, None), check_vma=False
    )
```

```python
import functools
import math

import jax
import jax.numpy as jnp
from jax import lax
from jax.experimental import pallas as pl
from jax.experimental.pallas import tpu as pltpu
from jax.sharding import Mesh
from jax.sharding import PartitionSpec as P

F32 = jnp.float32
BF16 = jnp.bfloat16
I32 = jnp.int32

C = 256
FH = 1024
FHEADS = 8
BALL = 256
POOL = 16
CC = 1024
N_DEV = 128
CAP = 16
PTS = 1024
SLOTS = N_DEV * CAP
CROWS = PTS // POOL
N_BALL = 16
N_Z = 4
N_HID = 8
EPS = 1e-06
LOG2E = 1.4426950408889634
ALL = ("ball", "z", "core")
VMEM_LIMIT = 56 * 2**20

NT = (((1,), (1,)), ((), ()))


def params():
    return pltpu.CompilerParams(vmem_limit_bytes=VMEM_LIMIT)


def iota(shape, dim):
    return lax.broadcasted_iota(I32, shape, dim)


def onehot(mask):
    return jnp.where(mask, 1.0, 0.0).astype(BF16)


def mm(a, b):
    return jnp.dot(a, b, preferred_element_type=F32)


def mm_nt(a, b):
    return lax.dot_general(a, b, NT, preferred_element_type=F32)


def rms(values, gain):
    mean_square = jnp.mean(values * values, axis=-1, keepdims=True)
    return (values * lax.rsqrt(mean_square + EPS) * gain).astype(BF16)


def silu(v):
    return 0.5 * v * (1.0 + jnp.tanh(0.5 * v))


def slice_kernel(at_ball, gate_up, down, pool, unpool, qkv, out, mlp, piece):
    mlp[0:64, :] = gate_up[0]
    mlp[64:128, :] = gate_up[1]
    mlp[128:160, :] = down[:, :512]
    mlp[160:192, :] = down[:, 512:]
    piece[0:32, :] = pool[:, :512]
    piece[32:64, :] = pool[:, 512:]
    piece[64:128, :] = unpool[...]
    for part in range(4):
        rows = slice(16 * part, 16 * part + 16)
        lanes = slice(128 * part, 128 * part + 128)
        for which in range(3):
            piece[128 + 16 * which : 144 + 16 * which, lanes] = qkv[which, rows, :]
        piece[176:192, lanes] = out[rows, :]


def prep_kernel(points, tree, rot, send, slots):
    upper = onehot(iota((PTS, PTS), 0) < iota((PTS, PTS), 1))
    device = iota((N_DEV, PTS), 0)
    digits = []
    for which, ref in ((0, tree), (1, rot)):
        target = ref[...]
        owner = target >> 10
        within = (target & (PTS - 1)) + 1
        match = jnp.where(device == owner, 1.0, 0.0)
        before = mm(match.astype(BF16), upper)
        rank = jnp.sum(match * before, axis=0, keepdims=True).astype(I32)
        slots[which : which + 1, :] = owner * CAP + rank
        row = device - 2 * which
        high = (within >> 5).astype(F32)
        low = (within & 31).astype(F32)
        digits.append(jnp.where(row == 0, high, jnp.where(row == 1, low, 0.0)).astype(BF16))
    for chunk in range(SLOTS // 256):
        rows = slice(chunk * 256, (chunk + 1) * 256)
        slot = iota((256, PTS), 0) + chunk * 256
        tree_pick = onehot(slot == slots[0:1, :])
        rot_pick = onehot(slot == slots[1:2, :])
        send[rows, :C] = mm(tree_pick, points[...]).astype(BF16)
        send[rows, C:] = (mm_nt(tree_pick, digits[0]) + mm_nt(rot_pick, digits[1])).astype(BF16)


def pack(slot_row, source, send):
    for chunk in range(SLOTS // 256):
        pick = onehot(iota((256, PTS), 0) + chunk * 256 == slot_row)
        send[chunk * 256 : (chunk + 1) * 256, :] = mm(pick, source[...]).astype(BF16)


def fine_ball(x_16, gains, qkv, out, gate_up, down):
    x = x_16.astype(F32)
    normed = rms(x, gains[0, 0:1, :])
    q = mm(normed, qkv[0, 0]).astype(BF16)
    k = mm(normed, qkv[0, 1]).astype(BF16)
    v = mm(normed, qkv[0, 2]).astype(BF16)
    width = C // FHEADS
    head_of = iota((BALL, C), 1) // width
    scale = LOG2E / math.sqrt(width)
    mixed = jnp.zeros((BALL, C), F32)
    inverse = jnp.zeros((BALL, C), F32)
    zero = jnp.zeros((BALL, C), BF16)
    for head in range(FHEADS):
        mine = head_of == head
        scores = mm_nt(q, jnp.where(mine, k, zero))
        top = jnp.max(scores, axis=-1, keepdims=True)
        weights = jnp.exp2((scores - top) * scale)
        total = jnp.sum(weights, axis=-1, keepdims=True)
        mixed = mixed + mm(weights.astype(BF16), jnp.where(mine, v, zero))
        inverse = jnp.where(mine, 1.0 / total, inverse)
    mixed = (mixed * inverse).astype(BF16)
    attended = (x + mm(mixed, out[0])).astype(BF16).astype(F32)
    normed = rms(attended, gains[0, 1:2, :])
    hidden = (silu(mm(normed, gate_up[0, 0])) * mm(normed, gate_up[0, 1])).astype(BF16)
    return (attended + mm(hidden, down[0])).astype(BF16)


def fine_kernel(which, rows, place, slots, gains, qkv, out, gate_up, down, send, place_row, states):
    row = iota((8, N_DEV), 0)
    lane = iota((8, N_DEV), 1)
    digit = jnp.where(row == 0, jnp.where(lane == 2 * which, 32.0, 0.0), 0.0)
    digit = jnp.where((row == 0) & (lane == 2 * which + 1), 1.0, digit).astype(BF16)
    place_row[...] = mm_nt(digit, place[...]).astype(I32) - 1

    def one_ball(ball, carry):
        start = pl.multiple_of(ball * BALL, BALL)
        pick = onehot(iota((BALL, SLOTS), 0) + ball * BALL == place_row[0:1, :])
        x = mm(pick, rows[...]).astype(BF16)
        states[pl.ds(start, BALL), :] = fine_ball(x, gains, qkv, out, gate_up, down)
        return carry

    lax.fori_loop(0, PTS // BALL, one_ball, 0)

    if which == 0:
        pack(slots[1:2, :], states, send)
        return
    for chunk in range(SLOTS // 256):
        digits = place[chunk * 256 : (chunk + 1) * 256, :].astype(F32)
        at = (digits[:, 2:3] * 32.0 + digits[:, 3:4]).astype(I32) - 1
        pick = onehot(iota((256, PTS), 1) == at)
        send[chunk * 256 : (chunk + 1) * 256, :] = mm(pick, states[...]).astype(BF16)


def pool_kernel(returned, slots, pool, block_two, coarse, total):
    step = pl.program_id(0)
    slot = slots[1:2, :]
    high = (slot >> 5).astype(F32)
    low = (slot & 31).astype(F32)
    row = iota((8, PTS), 0)
    digits = jnp.where(row == 0, high, jnp.where(row == 1, low, 0.0)).astype(BF16)
    child = iota((128, PTS), 0)
    order = onehot(iota((128, PTS), 1) == POOL * (child & 63) + 2 * step + (child >> 6))
    found = mm_nt(order, digits)
    at = (found[:, 0:1] * 32.0 + found[:, 1:2]).astype(I32)
    pick = onehot(iota((128, SLOTS), 1) == at)
    two = mm(pick, returned[...]).astype(BF16)
    block_two[...] = two

    @pl.when(step == 0)
    def _():
        total[...] = jnp.zeros_like(total)

    for half in range(2):
        rows = slice(32 * half, 32 * half + 32)
        lanes = slice(512 * half, 512 * half + 512)
        weight = pool[:, 0, rows, :].reshape(512, 512)
        total[:, lanes] += mm(two[:CROWS], weight[:C]) + mm(two[CROWS:], weight[C:])

    @pl.when(step == N_HID - 1)
    def _():
        coarse[...] = total[...].astype(BF16)


def attn_kernel(own, from_z, pair, pair_z, gains, heads, mid, normed, rows_16, total, out):
    step = pl.program_id(0)

    @pl.when(step == 0)
    def _():
        for at, ref in enumerate((own, from_z, pair, pair_z)):
            values = ref[...].astype(F32)
            rows_16[CROWS * at : CROWS * at + CROWS, :] = rms(values, gains[0:1, :])
            total[CROWS * at : CROWS * at + CROWS, :] = values

    def weight(which):
        rows = slice(16 * which, 16 * which + 16)
        return jnp.stack(
            [heads[:, 0, rows, 128 * part : 128 * part + 128] for part in range(4)], axis=1
        ).reshape(CC, 128)

    for ball in range(N_BALL):
        lanes = slice(128 * (ball % 8), 128 * (ball % 8) + 128)
        for part in range(4):
            top = 64 * (ball // 8) + 16 * part
            out[top : top + 16, lanes] = heads[ball, 0, 48:64, 128 * part : 128 * part + 128]

    rows = rows_16[...]
    q = mm(rows, weight(0)).astype(BF16)
    k = mm(rows, weight(1)).astype(BF16)
    v = mm(rows, weight(2)).astype(BF16)
    head_of = iota((BALL, 128), 1) // 64
    scale = LOG2E / math.sqrt(64)
    mixed = jnp.zeros((BALL, 128), F32)
    inverse = jnp.zeros((BALL, 128), F32)
    zero = jnp.zeros((BALL, 128), BF16)
    for head in range(2):
        mine = head_of == head
        scores = mm_nt(q, jnp.where(mine, k, zero))
        top = jnp.max(scores, axis=-1, keepdims=True)
        weights = jnp.exp2((scores - top) * scale)
        sums = jnp.sum(weights, axis=-1, keepdims=True)
        mixed = mixed + mm(weights.astype(BF16), jnp.where(mine, v, zero))
        inverse = jnp.where(mine, 1.0 / sums, inverse)
    total[...] += mm((mixed * inverse).astype(BF16), out[...])

    @pl.when(step == N_HID - 1)
    def _():
        values = total[...].astype(BF16)
        mid[...] = values[:CROWS]
        normed[...] = rms(values.astype(F32), gains[1:2, :])


def mlp_kernel(normed, own_gate_up, own_down, far_gate, far_up, far_down, kept, kept_z, sent, total):
    step = pl.program_id(0)

    def hidden_of(gate, up):
        rows = normed[...]
        return (silu(mm(rows, gate)) * mm(rows, up)).astype(BF16)

    @pl.when(step == 0)
    def _():
        total[...] = jnp.zeros_like(total)

    @pl.when(step < 2)
    def _():
        total[...] += mm(hidden_of(own_gate_up[0], own_gate_up[1]), own_down[...])

    @pl.when(step >= 2)
    def _():
        hidden = hidden_of(far_gate[...].reshape(CC, 256), far_up[...].reshape(CC, 256))
        total[:, :512] += mm(hidden, far_down[:, :32, :].reshape(256, 512))
        total[:, 512:] += mm(hidden, far_down[:, 32:, :].reshape(256, 512))

    @pl.when(step == 3)
    def _():
        kept[...] = total[:CROWS, :]
        kept_z[...] = total[CROWS : 2 * CROWS, :]
        sent[...] = total[2 * CROWS :, :].astype(BF16)


def unpool_kernel(mid, kept, got, got_z, unpool, block_two, joined, done, children):
    step = pl.program_id(0)

    @pl.when(step == 0)
    def _():
        parts = kept[...] + got[...].astype(F32) + got_z[...].astype(F32)
        done[...] = (mid[...].astype(F32) + parts).astype(BF16)

    spread = mm(done[...], unpool[...].reshape(CC, 512)).astype(BF16).astype(F32)
    start = pl.multiple_of(step * 128, 128)
    two = block_two[...].astype(F32)
    children[pl.ds(start, CROWS), :] = (two[:CROWS] + spread[:, :C]).astype(BF16)
    children[pl.ds(start + CROWS, CROWS), :] = (two[CROWS:] + spread[:, C:]).astype(BF16)

    @pl.when(step == N_HID - 1)
    def _():
        for chunk in range(4):
            point = iota((256, PTS), 0) + chunk * 256
            child = iota((256, PTS), 1)
            order = onehot(point == POOL * (child & 63) + (child >> 6))
            joined[chunk * 256 : (chunk + 1) * 256, :] = mm(order, children[...]).astype(BF16)


def shape(dims, dtype):
    return jax.ShapeDtypeStruct(dims, dtype)


def whole(dims):
    zeros = (0,) * len(dims)
    return pl.BlockSpec(dims, lambda *_: zeros)


def layer(dims, which):
    index = (which,) + (0,) * (len(dims) - 1)
    return pl.BlockSpec((1,) + dims[1:], lambda *_: index)


def unit(which):
    return pl.BlockSpec(
        (N_BALL, 1, 64, 512), lambda i: (0, jnp.minimum(i, N_HID - 1), which, 0)
    )


def hidden_half(first, gate_up):
    if gate_up:
        return pl.BlockSpec((2, CC, 256), lambda i: (0, 0, jnp.clip(i - first, 0, 1)))
    return pl.BlockSpec((256, CC), lambda i: (jnp.clip(i - first, 0, 1), 0))


def far_halves(first):
    def half(i):
        return jnp.clip(i - first, 0, 1)

    return (
        pl.BlockSpec((N_BALL, 64, 256), lambda i: (0, 0, half(i))),
        pl.BlockSpec((N_BALL, 64, 256), lambda i: (0, 1, half(i))),
        pl.BlockSpec((N_BALL // 2, 64, 512), lambda i: (half(i), 2, 0)),
    )


def exchange(values):
    return lax.all_to_all(values, ALL, split_axis=0, concat_axis=0, tiled=True)


def other_core(values):
    return lax.ppermute(values, "core", [(0, 1), (1, 0)])


def other_z(values):
    return lax.ppermute(values, "z", [(0, 1), (1, 0), (2, 3), (3, 2)])


def far_z(values):
    return lax.ppermute(values, "z", [(0, 3), (3, 0), (1, 2), (2, 1)])


def fine(which, rows, place, slots, norm, qkv, out, gate_up, down):
    return pl.pallas_call(
        functools.partial(fine_kernel, which),
        grid=(1,),
        out_shape=shape((SLOTS, C), BF16),
        in_specs=[
            whole((SLOTS, C)),
            pl.BlockSpec((SLOTS, N_DEV), lambda i: (0, 2)),
            whole((2, PTS)),
            layer(norm.shape, which),
            layer(qkv.shape, which),
            layer(out.shape, which),
            layer(gate_up.shape, which),
            layer(down.shape, which),
        ],
        out_specs=whole((SLOTS, C)),
        scratch_shapes=[pltpu.VMEM((8, SLOTS), I32), pltpu.VMEM((PTS, C), BF16)],
        compiler_params=params(),
        cost_estimate=pl.CostEstimate(flops=8 * 10**9, bytes_accessed=4 * 2**20, transcendentals=0),
        name=f"fine_block_{which}",
    )(rows, place, slots, norm, qkv, out, gate_up, down)


def body(
    points,
    tree_slot,
    rotated_slot,
    fine_norm,
    fine_qkv,
    fine_out,
    fine_gate_up,
    fine_down,
    pool_weight,
    coarse_norm,
    coarse_qkv,
    coarse_out,
    coarse_gate_up,
    coarse_down,
    unpool_weight,
):
    mlp_piece, piece = pl.pallas_call(
        slice_kernel,
        grid_spec=pltpu.PrefetchScalarGridSpec(
            num_scalar_prefetch=1,
            grid=(1,),
            in_specs=[
                pl.BlockSpec((2, 64, 512), lambda i, at: (0, at[0], 0)),
                pl.BlockSpec((32, CC), lambda i, at: (at[0], 0)),
                pl.BlockSpec((32, CC), lambda i, at: (at[0], 0)),
                pl.BlockSpec((64, 512), lambda i, at: (at[0], 0)),
                pl.BlockSpec((3, 64, 128), lambda i, at: (0, at[0], 0)),
                pl.BlockSpec((64, 128), lambda i, at: (at[0] // 8, at[0] % 8)),
            ],
            out_specs=(pl.BlockSpec((192, 512), lambda i, at: (0, 0)),) * 2,
        ),
        out_shape=(shape((192, 512), BF16),) * 2,
        compiler_params=params(),
        name="cut",
    )(
        lax.axis_index("ball").reshape(1),
        coarse_gate_up,
        coarse_down,
        pool_weight,
        unpool_weight,
        coarse_qkv,
        coarse_out,
    )
    weights = lax.all_gather(piece, ALL).reshape(N_BALL, N_HID, 192, 512)

    send, slots = pl.pallas_call(
        prep_kernel,
        out_shape=(shape((SLOTS, C + N_DEV), BF16), shape((2, PTS), I32)),
        compiler_params=params(),
        cost_estimate=pl.CostEstimate(flops=6 * 10**9, bytes_accessed=2 * 2**20, transcendentals=0),
        name="prep",
    )(points, tree_slot.reshape(1, PTS), rotated_slot.reshape(1, PTS))
    far_piece, send = lax.optimization_barrier((far_z(mlp_piece), send))
    far_mlp = lax.all_gather(far_piece, "ball")
    first = exchange(send)
    fine_weights = (fine_norm, fine_qkv, fine_out, fine_gate_up, fine_down)
    rows = exchange(fine(0, first, first, slots, *fine_weights))
    returned = exchange(fine(1, rows, first, slots, *fine_weights))

    block_two, coarse = pl.pallas_call(
        pool_kernel,
        grid=(N_HID,),
        out_shape=(shape((PTS, C), BF16), shape((CROWS, CC), BF16)),
        in_specs=[whole((SLOTS, C)), whole((2, PTS)), unit(0)],
        out_specs=(pl.BlockSpec((128, C), lambda i: (i, 0)), whole((CROWS, CC))),
        scratch_shapes=[pltpu.VMEM((CROWS, CC), F32)],
        compiler_params=params(),
        name="pool",
    )(returned, slots, weights)

    from_z = other_z(coarse)
    rows_64 = whole((CROWS, CC))
    mid, normed = pl.pallas_call(
        attn_kernel,
        grid=(N_HID,),
        out_shape=(shape((CROWS, CC), BF16), shape((4 * CROWS, CC), BF16)),
        in_specs=[rows_64, rows_64, rows_64, rows_64, whole((2, CC)), unit(2)],
        out_specs=(rows_64, whole((4 * CROWS, CC))),
        scratch_shapes=[
            pltpu.VMEM((4 * CROWS, CC), BF16),
            pltpu.VMEM((4 * CROWS, CC), F32),
            pltpu.VMEM((128, CC), BF16),
        ],
        compiler_params=params(),
        name="attn",
    )(coarse, from_z, other_core(coarse), other_core(from_z), coarse_norm, weights)

    kept, kept_z, sent = pl.pallas_call(
        mlp_kernel,
        grid=(4,),
        out_shape=(
            shape((CROWS, CC), F32),
            shape((CROWS, CC), F32),
            shape((2 * CROWS, CC), BF16),
        ),
        in_specs=[
            whole((4 * CROWS, CC)),
            hidden_half(0, True),
            hidden_half(0, False),
            *far_halves(2),
        ],
        out_specs=(rows_64, rows_64, whole((2 * CROWS, CC))),
        scratch_shapes=[pltpu.VMEM((4 * CROWS, CC), F32)],
        compiler_params=params(),
        name="mlp",
    )(normed, coarse_gate_up, coarse_down, far_mlp, far_mlp, far_mlp)

    got = other_core(sent)
    got_z = other_z((kept_z + got[CROWS:].astype(F32)).astype(BF16))
    return pl.pallas_call(
        unpool_kernel,
        grid=(N_HID,),
        out_shape=shape((PTS, C), BF16),
        in_specs=[
            rows_64,
            rows_64,
            rows_64,
            rows_64,
            unit(1),
            pl.BlockSpec((128, C), lambda i: (i, 0)),
        ],
        out_specs=whole((PTS, C)),
        scratch_shapes=[pltpu.VMEM((CROWS, CC), BF16), pltpu.VMEM((PTS, C), BF16)],
        compiler_params=params(),
        name="unpool",
    )(mid, kept, got, got_z, weights, block_two)


def solution(mesh):
    split = Mesh(mesh.devices.reshape(N_BALL, N_Z, 2), ALL)
    hid = ("z", "core")
    placed = (
        P(ALL, None),
        P(ALL),
        P(ALL),
        P(),
        P(),
        P(),
        P(),
        P(),
        P(hid, None),
        P(),
        P(None, None, hid),
        P(hid, None),
        P(None, None, hid),
        P(hid, None),
        P(None, hid),
    )
    return jax.shard_map(
        body, mesh=split, in_specs=placed, out_specs=P(ALL, None), check_vma=False
    )
```

```python
import functools
import math

import jax
import jax.numpy as jnp
from jax import lax
from jax.experimental import pallas as pl
from jax.experimental.pallas import tpu as pltpu
from jax.sharding import Mesh
from jax.sharding import PartitionSpec as P

F32 = jnp.float32
BF16 = jnp.bfloat16
I32 = jnp.int32

C = 256
FH = 1024
FHEADS = 8
BALL = 256
POOL = 16
CC = 1024
N_DEV = 128
CAP = 16
PTS = 1024
SLOTS = N_DEV * CAP
CROWS = PTS // POOL
N_BALL = 16
N_Z = 4
N_HID = 8
EPS = 1e-06
LOG2E = 1.4426950408889634
ALL = ("ball", "z", "core")
VMEM_LIMIT = 56 * 2**20

NT = (((1,), (1,)), ((), ()))


def params():
    return pltpu.CompilerParams(vmem_limit_bytes=VMEM_LIMIT)


def iota(shape, dim):
    return lax.broadcasted_iota(I32, shape, dim)


def onehot(mask):
    return jnp.where(mask, 1.0, 0.0).astype(BF16)


def mm(a, b):
    return jnp.dot(a, b, preferred_element_type=F32)


def mm_nt(a, b):
    return lax.dot_general(a, b, NT, preferred_element_type=F32)


def rms(values, gain):
    mean_square = jnp.mean(values * values, axis=-1, keepdims=True)
    return (values * lax.rsqrt(mean_square + EPS) * gain).astype(BF16)


def silu(v):
    return 0.5 * v * (1.0 + jnp.tanh(0.5 * v))


def slice_kernel(at_ball, gate_up, down, pool, unpool, qkv, out, mlp, piece):
    mlp[0:64, :] = gate_up[0]
    mlp[64:128, :] = gate_up[1]
    mlp[128:160, :] = down[:, :512]
    mlp[160:192, :] = down[:, 512:]
    piece[0:32, :] = pool[:, :512]
    piece[32:64, :] = pool[:, 512:]
    piece[64:128, :] = unpool[...]
    for part in range(4):
        rows = slice(16 * part, 16 * part + 16)
        lanes = slice(128 * part, 128 * part + 128)
        for which in range(3):
            piece[128 + 16 * which : 144 + 16 * which, lanes] = qkv[which, rows, :]
        piece[176:192, lanes] = out[rows, :]


def prep_kernel(points, tree, rot, send, slots):
    upper = onehot(iota((PTS, PTS), 0) < iota((PTS, PTS), 1))
    device = iota((N_DEV, PTS), 0)
    digits = []
    for which, ref in ((0, tree), (1, rot)):
        target = ref[...]
        owner = target >> 10
        within = (target & (PTS - 1)) + 1
        match = jnp.where(device == owner, 1.0, 0.0)
        before = mm(match.astype(BF16), upper)
        rank = jnp.sum(match * before, axis=0, keepdims=True).astype(I32)
        slots[which : which + 1, :] = owner * CAP + rank
        row = device - 2 * which
        high = (within >> 5).astype(F32)
        low = (within & 31).astype(F32)
        digits.append(jnp.where(row == 0, high, jnp.where(row == 1, low, 0.0)).astype(BF16))
    for chunk in range(SLOTS // 256):
        rows = slice(chunk * 256, (chunk + 1) * 256)
        slot = iota((256, PTS), 0) + chunk * 256
        tree_pick = onehot(slot == slots[0:1, :])
        rot_pick = onehot(slot == slots[1:2, :])
        send[rows, :C] = mm(tree_pick, points[...]).astype(BF16)
        send[rows, C:] = (mm_nt(tree_pick, digits[0]) + mm_nt(rot_pick, digits[1])).astype(BF16)


def pack(slot_row, source, send):
    for chunk in range(SLOTS // 256):
        pick = onehot(iota((256, PTS), 0) + chunk * 256 == slot_row)
        send[chunk * 256 : (chunk + 1) * 256, :] = mm(pick, source[...]).astype(BF16)


def fine_ball(x_16, gains, qkv, out, gate_up, down):
    x = x_16.astype(F32)
    normed = rms(x, gains[0, 0:1, :])
    q = mm(normed, qkv[0, 0]).astype(BF16)
    k = mm(normed, qkv[0, 1]).astype(BF16)
    v = mm(normed, qkv[0, 2]).astype(BF16)
    width = C // FHEADS
    head_of = iota((BALL, C), 1) // width
    scale = LOG2E / math.sqrt(width)
    mixed = jnp.zeros((BALL, C), F32)
    inverse = jnp.zeros((BALL, C), F32)
    zero = jnp.zeros((BALL, C), BF16)
    for head in range(FHEADS):
        mine = head_of == head
        scores = mm_nt(q, jnp.where(mine, k, zero))
        top = jnp.max(scores, axis=-1, keepdims=True)
        weights = jnp.exp2((scores - top) * scale)
        total = jnp.sum(weights, axis=-1, keepdims=True)
        mixed = mixed + mm(weights.astype(BF16), jnp.where(mine, v, zero))
        inverse = jnp.where(mine, 1.0 / total, inverse)
    mixed = (mixed * inverse).astype(BF16)
    attended = (x + mm(mixed, out[0])).astype(BF16).astype(F32)
    normed = rms(attended, gains[0, 1:2, :])
    hidden = (silu(mm(normed, gate_up[0, 0])) * mm(normed, gate_up[0, 1])).astype(BF16)
    return (attended + mm(hidden, down[0])).astype(BF16)


def fine_kernel(which, rows, place, slots, gains, qkv, out, gate_up, down, send, place_row, states):
    row = iota((8, N_DEV), 0)
    lane = iota((8, N_DEV), 1)
    digit = jnp.where(row == 0, jnp.where(lane == 2 * which, 32.0, 0.0), 0.0)
    digit = jnp.where((row == 0) & (lane == 2 * which + 1), 1.0, digit).astype(BF16)
    place_row[...] = mm_nt(digit, place[...]).astype(I32) - 1

    def one_ball(ball, carry):
        start = pl.multiple_of(ball * BALL, BALL)
        pick = onehot(iota((BALL, SLOTS), 0) + ball * BALL == place_row[0:1, :])
        x = mm(pick, rows[...]).astype(BF16)
        states[pl.ds(start, BALL), :] = fine_ball(x, gains, qkv, out, gate_up, down)
        return carry

    lax.fori_loop(0, PTS // BALL, one_ball, 0, unroll=True)

    if which == 0:
        pack(slots[1:2, :], states, send)
        return
    for chunk in range(SLOTS // 256):
        digits = place[chunk * 256 : (chunk + 1) * 256, :].astype(F32)
        at = (digits[:, 2:3] * 32.0 + digits[:, 3:4]).astype(I32) - 1
        pick = onehot(iota((256, PTS), 1) == at)
        send[chunk * 256 : (chunk + 1) * 256, :] = mm(pick, states[...]).astype(BF16)


def pool_kernel(returned, slots, pool, block_two, coarse, total):
    step = pl.program_id(0)
    slot = slots[1:2, :]
    high = (slot >> 5).astype(F32)
    low = (slot & 31).astype(F32)
    row = iota((8, PTS), 0)
    digits = jnp.where(row == 0, high, jnp.where(row == 1, low, 0.0)).astype(BF16)
    child = iota((128, PTS), 0)
    order = onehot(iota((128, PTS), 1) == POOL * (child & 63) + 2 * step + (child >> 6))
    found = mm_nt(order, digits)
    at = (found[:, 0:1] * 32.0 + found[:, 1:2]).astype(I32)
    pick = onehot(iota((128, SLOTS), 1) == at)
    two = mm(pick, returned[...]).astype(BF16)
    block_two[...] = two

    @pl.when(step == 0)
    def _():
        total[...] = jnp.zeros_like(total)

    for half in range(2):
        rows = slice(32 * half, 32 * half + 32)
        lanes = slice(512 * half, 512 * half + 512)
        weight = pool[:, 0, rows, :].reshape(512, 512)
        total[:, lanes] += mm(two[:CROWS], weight[:C]) + mm(two[CROWS:], weight[C:])

    @pl.when(step == N_HID - 1)
    def _():
        coarse[...] = total[...].astype(BF16)


def attn_kernel(own, from_z, pair, pair_z, gains, heads, gate_up, down, mid, normed, partial, rows_16, total, out):
    step = pl.program_id(0)

    @pl.when(step == 0)
    def _():
        for at, ref in enumerate((own, from_z, pair, pair_z)):
            values = ref[...].astype(F32)
            rows_16[CROWS * at : CROWS * at + CROWS, :] = rms(values, gains[0:1, :])
            total[CROWS * at : CROWS * at + CROWS, :] = values

    @pl.when(step < N_HID)
    def _():
        def weight(which):
            rows = slice(16 * which, 16 * which + 16)
            return jnp.stack(
                [heads[:, 0, rows, 128 * part : 128 * part + 128] for part in range(4)], axis=1
            ).reshape(CC, 128)

        for ball in range(N_BALL):
            lanes = slice(128 * (ball % 8), 128 * (ball % 8) + 128)
            for part in range(4):
                top = 64 * (ball // 8) + 16 * part
                out[top : top + 16, lanes] = heads[ball, 0, 48:64, 128 * part : 128 * part + 128]

        rows = rows_16[...]
        q = mm(rows, weight(0)).astype(BF16)
        k = mm(rows, weight(1)).astype(BF16)
        v = mm(rows, weight(2)).astype(BF16)
        head_of = iota((BALL, 128), 1) // 64
        scale = LOG2E / math.sqrt(64)
        mixed = jnp.zeros((BALL, 128), F32)
        inverse = jnp.zeros((BALL, 128), F32)
        zero = jnp.zeros((BALL, 128), BF16)
        for head in range(2):
            mine = head_of == head
            scores = mm_nt(q, jnp.where(mine, k, zero))
            top = jnp.max(scores, axis=-1, keepdims=True)
            weights = jnp.exp2((scores - top) * scale)
            sums = jnp.sum(weights, axis=-1, keepdims=True)
            mixed = mixed + mm(weights.astype(BF16), jnp.where(mine, v, zero))
            inverse = jnp.where(mine, 1.0 / sums, inverse)
        total[...] += mm((mixed * inverse).astype(BF16), out[...])

    @pl.when(step == N_HID)
    def _():
        values = total[...].astype(BF16)
        mid[...] = values[:CROWS]
        normed[...] = rms(values.astype(F32), gains[1:2, :])
        partial[...] = jnp.zeros_like(partial)

    @pl.when(step >= N_HID)
    def _():
        partial[...] += mm(hidden_of(normed[...], gate_up[0], gate_up[1]), down[...])


def hidden_of(rows, gate, up):
    return (silu(mm(rows, gate)) * mm(rows, up)).astype(BF16)


def mlp_kernel(normed, partial, gate, up, down, kept, kept_z, sent, total):
    step = pl.program_id(0)

    @pl.when(step == 0)
    def _():
        total[...] = partial[...]

    hidden = hidden_of(normed[...], gate[...].reshape(CC, 256), up[...].reshape(CC, 256))
    total[:, :512] += mm(hidden, down[:, :32, :].reshape(256, 512))
    total[:, 512:] += mm(hidden, down[:, 32:, :].reshape(256, 512))

    @pl.when(step == 1)
    def _():
        kept[...] = total[:CROWS, :]
        kept_z[...] = total[CROWS : 2 * CROWS, :]
        sent[...] = total[2 * CROWS :, :].astype(BF16)


def unpool_kernel(mid, kept, got, got_z, unpool, block_two, joined, done, children):
    step = pl.program_id(0)

    @pl.when(step == 0)
    def _():
        parts = kept[...] + got[...].astype(F32) + got_z[...].astype(F32)
        done[...] = (mid[...].astype(F32) + parts).astype(BF16)

    spread = mm(done[...], unpool[...].reshape(CC, 512)).astype(BF16).astype(F32)
    start = pl.multiple_of(step * 128, 128)
    two = block_two[...].astype(F32)
    children[pl.ds(start, CROWS), :] = (two[:CROWS] + spread[:, :C]).astype(BF16)
    children[pl.ds(start + CROWS, CROWS), :] = (two[CROWS:] + spread[:, C:]).astype(BF16)

    @pl.when(step == N_HID - 1)
    def _():
        for chunk in range(4):
            point = iota((256, PTS), 0) + chunk * 256
            child = iota((256, PTS), 1)
            order = onehot(point == POOL * (child & 63) + (child >> 6))
            joined[chunk * 256 : (chunk + 1) * 256, :] = mm(order, children[...]).astype(BF16)


def shape(dims, dtype):
    return jax.ShapeDtypeStruct(dims, dtype)


def whole(dims):
    zeros = (0,) * len(dims)
    return pl.BlockSpec(dims, lambda *_: zeros)


def layer(dims, which):
    index = (which,) + (0,) * (len(dims) - 1)
    return pl.BlockSpec((1,) + dims[1:], lambda *_: index)


def unit(which):
    return pl.BlockSpec(
        (N_BALL, 1, 64, 512), lambda i: (0, jnp.minimum(i, N_HID - 1), which, 0)
    )


def hidden_half(first, gate_up):
    if gate_up:
        return pl.BlockSpec((2, CC, 256), lambda i: (0, 0, jnp.clip(i - first, 0, 1)))
    return pl.BlockSpec((256, CC), lambda i: (jnp.clip(i - first, 0, 1), 0))


def far_halves(first):
    def half(i):
        return jnp.clip(i - first, 0, 1)

    return (
        pl.BlockSpec((N_BALL, 64, 256), lambda i: (0, 0, half(i))),
        pl.BlockSpec((N_BALL, 64, 256), lambda i: (0, 1, half(i))),
        pl.BlockSpec((N_BALL // 2, 64, 512), lambda i: (half(i), 2, 0)),
    )


def exchange(values):
    return lax.all_to_all(values, ALL, split_axis=0, concat_axis=0, tiled=True)


def other_core(values):
    return lax.ppermute(values, "core", [(0, 1), (1, 0)])


def other_z(values):
    return lax.ppermute(values, "z", [(0, 1), (1, 0), (2, 3), (3, 2)])


def far_z(values):
    return lax.ppermute(values, "z", [(0, 3), (3, 0), (1, 2), (2, 1)])


def fine(which, rows, place, slots, norm, qkv, out, gate_up, down):
    return pl.pallas_call(
        functools.partial(fine_kernel, which),
        grid=(1,),
        out_shape=shape((SLOTS, C), BF16),
        in_specs=[
            whole((SLOTS, C)),
            pl.BlockSpec((SLOTS, N_DEV), lambda i: (0, 2)),
            whole((2, PTS)),
            layer(norm.shape, which),
            layer(qkv.shape, which),
            layer(out.shape, which),
            layer(gate_up.shape, which),
            layer(down.shape, which),
        ],
        out_specs=whole((SLOTS, C)),
        scratch_shapes=[pltpu.VMEM((8, SLOTS), I32), pltpu.VMEM((PTS, C), BF16)],
        compiler_params=params(),
        cost_estimate=pl.CostEstimate(flops=8 * 10**9, bytes_accessed=4 * 2**20, transcendentals=0),
        name=f"fine_block_{which}",
    )(rows, place, slots, norm, qkv, out, gate_up, down)


def body(
    points,
    tree_slot,
    rotated_slot,
    fine_norm,
    fine_qkv,
    fine_out,
    fine_gate_up,
    fine_down,
    pool_weight,
    coarse_norm,
    coarse_qkv,
    coarse_out,
    coarse_gate_up,
    coarse_down,
    unpool_weight,
):
    mlp_piece, piece = pl.pallas_call(
        slice_kernel,
        grid_spec=pltpu.PrefetchScalarGridSpec(
            num_scalar_prefetch=1,
            grid=(1,),
            in_specs=[
                pl.BlockSpec((2, 64, 512), lambda i, at: (0, at[0], 0)),
                pl.BlockSpec((32, CC), lambda i, at: (at[0], 0)),
                pl.BlockSpec((32, CC), lambda i, at: (at[0], 0)),
                pl.BlockSpec((64, 512), lambda i, at: (at[0], 0)),
                pl.BlockSpec((3, 64, 128), lambda i, at: (0, at[0], 0)),
                pl.BlockSpec((64, 128), lambda i, at: (at[0] // 8, at[0] % 8)),
            ],
            out_specs=(pl.BlockSpec((192, 512), lambda i, at: (0, 0)),) * 2,
        ),
        out_shape=(shape((192, 512), BF16),) * 2,
        compiler_params=params(),
        name="cut",
    )(
        lax.axis_index("ball").reshape(1),
        coarse_gate_up,
        coarse_down,
        pool_weight,
        unpool_weight,
        coarse_qkv,
        coarse_out,
    )
    weights = lax.all_gather(piece, ALL).reshape(N_BALL, N_HID, 192, 512)

    send, slots = pl.pallas_call(
        prep_kernel,
        out_shape=(shape((SLOTS, C + N_DEV), BF16), shape((2, PTS), I32)),
        compiler_params=params(),
        cost_estimate=pl.CostEstimate(flops=6 * 10**9, bytes_accessed=2 * 2**20, transcendentals=0),
        name="prep",
    )(points, tree_slot.reshape(1, PTS), rotated_slot.reshape(1, PTS))
    first = exchange(send)
    fine_weights = (fine_norm, fine_qkv, fine_out, fine_gate_up, fine_down)
    rows = exchange(fine(0, first, first, slots, *fine_weights))
    mlp_piece, rows = lax.optimization_barrier((mlp_piece, rows))
    answers = fine(1, rows, first, slots, *fine_weights)
    far_piece, answers = lax.optimization_barrier((far_z(mlp_piece), answers))
    far_mlp = lax.all_gather(far_piece, "ball")
    returned = exchange(answers)

    block_two, coarse = pl.pallas_call(
        pool_kernel,
        grid=(N_HID,),
        out_shape=(shape((PTS, C), BF16), shape((CROWS, CC), BF16)),
        in_specs=[whole((SLOTS, C)), whole((2, PTS)), unit(0)],
        out_specs=(pl.BlockSpec((128, C), lambda i: (i, 0)), whole((CROWS, CC))),
        scratch_shapes=[pltpu.VMEM((CROWS, CC), F32)],
        compiler_params=params(),
        name="pool",
    )(returned, slots, weights)

    from_z = other_z(coarse)
    rows_64 = whole((CROWS, CC))
    rows_256 = whole((4 * CROWS, CC))
    mid, normed, partial = pl.pallas_call(
        attn_kernel,
        grid=(N_HID + 2,),
        out_shape=(
            shape((CROWS, CC), BF16),
            shape((4 * CROWS, CC), BF16),
            shape((4 * CROWS, CC), F32),
        ),
        in_specs=[
            rows_64,
            rows_64,
            rows_64,
            rows_64,
            whole((2, CC)),
            unit(2),
            hidden_half(N_HID, True),
            hidden_half(N_HID, False),
        ],
        out_specs=(rows_64, rows_256, rows_256),
        scratch_shapes=[
            pltpu.VMEM((4 * CROWS, CC), BF16),
            pltpu.VMEM((4 * CROWS, CC), F32),
            pltpu.VMEM((128, CC), BF16),
        ],
        compiler_params=params(),
        name="attn",
    )(
        coarse,
        from_z,
        other_core(coarse),
        other_core(from_z),
        coarse_norm,
        weights,
        coarse_gate_up,
        coarse_down,
    )

    kept, kept_z, sent = pl.pallas_call(
        mlp_kernel,
        grid=(2,),
        out_shape=(
            shape((CROWS, CC), F32),
            shape((CROWS, CC), F32),
            shape((2 * CROWS, CC), BF16),
        ),
        in_specs=[rows_256, rows_256, *far_halves(0)],
        out_specs=(rows_64, rows_64, whole((2 * CROWS, CC))),
        scratch_shapes=[pltpu.VMEM((4 * CROWS, CC), F32)],
        compiler_params=params(),
        name="mlp",
    )(normed, partial, far_mlp, far_mlp, far_mlp)

    got = other_core(sent)
    got_z = other_z((kept_z + got[CROWS:].astype(F32)).astype(BF16))
    return pl.pallas_call(
        unpool_kernel,
        grid=(N_HID,),
        out_shape=shape((PTS, C), BF16),
        in_specs=[
            rows_64,
            rows_64,
            rows_64,
            rows_64,
            unit(1),
            pl.BlockSpec((128, C), lambda i: (i, 0)),
        ],
        out_specs=whole((PTS, C)),
        scratch_shapes=[pltpu.VMEM((CROWS, CC), BF16), pltpu.VMEM((PTS, C), BF16)],
        compiler_params=params(),
        name="unpool",
    )(mid, kept, got, got_z, weights, block_two)


def solution(mesh):
    split = Mesh(mesh.devices.reshape(N_BALL, N_Z, 2), ALL)
    hid = ("z", "core")
    placed = (
        P(ALL, None),
        P(ALL),
        P(ALL),
        P(),
        P(),
        P(),
        P(),
        P(),
        P(hid, None),
        P(),
        P(None, None, hid),
        P(hid, None),
        P(None, None, hid),
        P(hid, None),
        P(None, hid),
    )
    return jax.shard_map(
        body, mesh=split, in_specs=placed, out_specs=P(ALL, None), check_vma=False
    )
```

```python
import functools
import math

import jax
import jax.numpy as jnp
from jax import lax
from jax.experimental import pallas as pl
from jax.experimental.pallas import tpu as pltpu
from jax.sharding import Mesh
from jax.sharding import PartitionSpec as P

F32 = jnp.float32
BF16 = jnp.bfloat16
I32 = jnp.int32

C = 256
FH = 1024
FHEADS = 8
BALL = 256
POOL = 16
CC = 1024
N_DEV = 128
CAP = 16
PTS = 1024
SLOTS = N_DEV * CAP
CROWS = PTS // POOL
N_BALL = 16
N_Z = 4
N_HID = 8
STEPS = 4
EPS = 1e-06
LOG2E = 1.4426950408889634
ALL = ("ball", "z", "core")
VMEM_LIMIT = 56 * 2**20

NT = (((1,), (1,)), ((), ()))


def params():
    return pltpu.CompilerParams(vmem_limit_bytes=VMEM_LIMIT)


def iota(shape, dim):
    return lax.broadcasted_iota(I32, shape, dim)


def onehot(mask):
    return jnp.where(mask, 1.0, 0.0).astype(BF16)


def mm(a, b):
    return jnp.dot(a, b, preferred_element_type=F32)


def mm_nt(a, b):
    return lax.dot_general(a, b, NT, preferred_element_type=F32)


def rms(values, gain):
    mean_square = jnp.mean(values * values, axis=-1, keepdims=True)
    return (values * lax.rsqrt(mean_square + EPS) * gain).astype(BF16)


def silu(v):
    return 0.5 * v * (1.0 + jnp.tanh(0.5 * v))


def slice_kernel(at_ball, gate_up, down, pool, unpool, qkv, out, mlp, piece):
    mlp[0:64, :] = gate_up[0]
    mlp[64:128, :] = gate_up[1]
    mlp[128:160, :] = down[:, :512]
    mlp[160:192, :] = down[:, 512:]
    piece[0:32, :] = pool[:, :512]
    piece[32:64, :] = pool[:, 512:]
    piece[64:128, :] = unpool[...]
    for part in range(4):
        rows = slice(16 * part, 16 * part + 16)
        lanes = slice(128 * part, 128 * part + 128)
        for which in range(3):
            piece[128 + 16 * which : 144 + 16 * which, lanes] = qkv[which, rows, :]
        piece[176:192, lanes] = out[rows, :]


def prep_kernel(points, tree, rot, send, slots):
    upper = onehot(iota((PTS, PTS), 0) < iota((PTS, PTS), 1))
    device = iota((N_DEV, PTS), 0)
    digits = []
    for which, ref in ((0, tree), (1, rot)):
        target = ref[...]
        owner = target >> 10
        within = (target & (PTS - 1)) + 1
        match = jnp.where(device == owner, 1.0, 0.0)
        before = mm(match.astype(BF16), upper)
        rank = jnp.sum(match * before, axis=0, keepdims=True).astype(I32)
        slots[which : which + 1, :] = owner * CAP + rank
        row = device - 2 * which
        high = (within >> 5).astype(F32)
        low = (within & 31).astype(F32)
        digits.append(jnp.where(row == 0, high, jnp.where(row == 1, low, 0.0)).astype(BF16))
    for chunk in range(SLOTS // 256):
        rows = slice(chunk * 256, (chunk + 1) * 256)
        slot = iota((256, PTS), 0) + chunk * 256
        tree_pick = onehot(slot == slots[0:1, :])
        rot_pick = onehot(slot == slots[1:2, :])
        send[rows, :C] = mm(tree_pick, points[...]).astype(BF16)
        send[rows, C:] = (mm_nt(tree_pick, digits[0]) + mm_nt(rot_pick, digits[1])).astype(BF16)


def pack(slot_row, source, send):
    for chunk in range(SLOTS // 256):
        pick = onehot(iota((256, PTS), 0) + chunk * 256 == slot_row)
        send[chunk * 256 : (chunk + 1) * 256, :] = mm(pick, source[...]).astype(BF16)


def fine_ball(x_16, gains, qkv, out, gate_up, down):
    x = x_16.astype(F32)
    normed = rms(x, gains[0, 0:1, :])
    q = mm(normed, qkv[0, 0]).astype(BF16)
    k = mm(normed, qkv[0, 1]).astype(BF16)
    v = mm(normed, qkv[0, 2]).astype(BF16)
    width = C // FHEADS
    head_of = iota((BALL, C), 1) // width
    scale = LOG2E / math.sqrt(width)
    mixed = jnp.zeros((BALL, C), F32)
    inverse = jnp.zeros((BALL, C), F32)
    zero = jnp.zeros((BALL, C), BF16)
    for head in range(FHEADS):
        mine = head_of == head
        scores = mm_nt(q, jnp.where(mine, k, zero))
        top = jnp.max(scores, axis=-1, keepdims=True)
        weights = jnp.exp2((scores - top) * scale)
        total = jnp.sum(weights, axis=-1, keepdims=True)
        mixed = mixed + mm(weights.astype(BF16), jnp.where(mine, v, zero))
        inverse = jnp.where(mine, 1.0 / total, inverse)
    mixed = (mixed * inverse).astype(BF16)
    attended = (x + mm(mixed, out[0])).astype(BF16).astype(F32)
    normed = rms(attended, gains[0, 1:2, :])
    hidden = (silu(mm(normed, gate_up[0, 0])) * mm(normed, gate_up[0, 1])).astype(BF16)
    return (attended + mm(hidden, down[0])).astype(BF16)


def fine_kernel(which, rows, place, slots, gains, qkv, out, gate_up, down, send, place_row, states):
    row = iota((8, N_DEV), 0)
    lane = iota((8, N_DEV), 1)
    digit = jnp.where(row == 0, jnp.where(lane == 2 * which, 32.0, 0.0), 0.0)
    digit = jnp.where((row == 0) & (lane == 2 * which + 1), 1.0, digit).astype(BF16)
    place_row[...] = mm_nt(digit, place[...]).astype(I32) - 1

    def one_ball(ball, carry):
        start = pl.multiple_of(ball * BALL, BALL)
        pick = onehot(iota((BALL, SLOTS), 0) + ball * BALL == place_row[0:1, :])
        x = mm(pick, rows[...]).astype(BF16)
        states[pl.ds(start, BALL), :] = fine_ball(x, gains, qkv, out, gate_up, down)
        return carry

    lax.fori_loop(0, PTS // BALL, one_ball, 0, unroll=True)

    if which == 0:
        pack(slots[1:2, :], states, send)
        return
    for chunk in range(SLOTS // 256):
        digits = place[chunk * 256 : (chunk + 1) * 256, :].astype(F32)
        at = (digits[:, 2:3] * 32.0 + digits[:, 3:4]).astype(I32) - 1
        pick = onehot(iota((256, PTS), 1) == at)
        send[chunk * 256 : (chunk + 1) * 256, :] = mm(pick, states[...]).astype(BF16)


def pool_kernel(returned, slots, pool, block_two, coarse, total):
    step = pl.program_id(0)
    slot = slots[1:2, :]
    high = (slot >> 5).astype(F32)
    low = (slot & 31).astype(F32)
    row = iota((8, PTS), 0)
    digits = jnp.where(row == 0, high, jnp.where(row == 1, low, 0.0)).astype(BF16)
    child = iota((256, PTS), 0)
    order = onehot(iota((256, PTS), 1) == POOL * (child & 63) + 4 * step + (child >> 6))
    found = mm_nt(order, digits)
    at = (found[:, 0:1] * 32.0 + found[:, 1:2]).astype(I32)
    pick = onehot(iota((256, SLOTS), 1) == at)
    two = mm(pick, returned[...]).astype(BF16)
    block_two[...] = two
    grouped = jnp.concatenate([two[64 * at : 64 * at + 64] for at in range(4)], axis=1)

    @pl.when(step == 0)
    def _():
        total[...] = jnp.zeros_like(total)

    for half in range(2):
        rows = slice(32 * half, 32 * half + 32)
        lanes = slice(512 * half, 512 * half + 512)
        total[:, lanes] += mm(grouped[:, :512], pool[:, 0, rows, :].reshape(512, 512)) + mm(
            grouped[:, 512:], pool[:, 1, rows, :].reshape(512, 512)
        )

    @pl.when(step == STEPS - 1)
    def _():
        coarse[...] = total[...].astype(BF16)


def attn_kernel(own, from_z, pair, pair_z, gains, heads, gate_up, down, mid, normed, partial, rows_16, total, out):
    step = pl.program_id(0)

    @pl.when(step == 0)
    def _():
        for at, ref in enumerate((own, from_z, pair, pair_z)):
            values = ref[...].astype(F32)
            rows_16[CROWS * at : CROWS * at + CROWS, :] = rms(values, gains[0:1, :])
            total[CROWS * at : CROWS * at + CROWS, :] = values

    @pl.when(step < STEPS)
    def _():
        def weight(which):
            rows = slice(16 * which, 16 * which + 16)
            return jnp.concatenate(
                [
                    jnp.stack(
                        [heads[:, at, rows, 128 * part : 128 * part + 128] for part in range(4)],
                        axis=1,
                    ).reshape(CC, 128)
                    for at in range(2)
                ],
                axis=1,
            )

        for at in range(2):
            for ball in range(N_BALL):
                lanes = slice(128 * (ball % 8), 128 * (ball % 8) + 128)
                for part in range(4):
                    top = 128 * at + 64 * (ball // 8) + 16 * part
                    out[top : top + 16, lanes] = heads[
                        ball, at, 48:64, 128 * part : 128 * part + 128
                    ]

        rows = rows_16[...]
        q = mm(rows, weight(0)).astype(BF16)
        k = mm(rows, weight(1)).astype(BF16)
        v = mm(rows, weight(2)).astype(BF16)
        head_of = iota((BALL, 256), 1) // 64
        scale = LOG2E / math.sqrt(64)
        mixed = jnp.zeros((BALL, 256), F32)
        inverse = jnp.zeros((BALL, 256), F32)
        zero = jnp.zeros((BALL, 256), BF16)
        for head in range(4):
            mine = head_of == head
            scores = mm_nt(q, jnp.where(mine, k, zero))
            top = jnp.max(scores, axis=-1, keepdims=True)
            weights = jnp.exp2((scores - top) * scale)
            sums = jnp.sum(weights, axis=-1, keepdims=True)
            mixed = mixed + mm(weights.astype(BF16), jnp.where(mine, v, zero))
            inverse = jnp.where(mine, 1.0 / sums, inverse)
        total[...] += mm((mixed * inverse).astype(BF16), out[...])

    @pl.when(step == STEPS)
    def _():
        values = total[...].astype(BF16)
        mid[...] = values[:CROWS]
        normed[...] = rms(values.astype(F32), gains[1:2, :])
        partial[...] = jnp.zeros_like(partial)

    @pl.when(step >= STEPS)
    def _():
        partial[...] += mm(hidden_of(normed[...], gate_up[0], gate_up[1]), down[...])


def hidden_of(rows, gate, up):
    return (silu(mm(rows, gate)) * mm(rows, up)).astype(BF16)


def mlp_kernel(normed, partial, gate, up, down, kept, kept_z, sent, total):
    step = pl.program_id(0)

    @pl.when(step == 0)
    def _():
        total[...] = partial[...]

    hidden = hidden_of(normed[...], gate[...].reshape(CC, 256), up[...].reshape(CC, 256))
    total[:, :512] += mm(hidden, down[:, :32, :].reshape(256, 512))
    total[:, 512:] += mm(hidden, down[:, 32:, :].reshape(256, 512))

    @pl.when(step == 1)
    def _():
        kept[...] = total[:CROWS, :]
        kept_z[...] = total[CROWS : 2 * CROWS, :]
        sent[...] = total[2 * CROWS :, :].astype(BF16)


def unpool_kernel(mid, kept, got, got_z, unpool, block_two, joined, done, children):
    step = pl.program_id(0)

    @pl.when(step == 0)
    def _():
        parts = kept[...] + got[...].astype(F32) + got_z[...].astype(F32)
        done[...] = (mid[...].astype(F32) + parts).astype(BF16)

    two = block_two[...].astype(F32)
    for at in range(2):
        spread = mm(done[...], unpool[:, at].reshape(CC, 512)).astype(BF16).astype(F32)
        for half in range(2):
            top = 128 * at + 64 * half
            start = pl.multiple_of(step * 256 + top, 64)
            added = two[top : top + CROWS] + spread[:, C * half : C * half + C]
            children[pl.ds(start, CROWS), :] = added.astype(BF16)

    @pl.when(step == STEPS - 1)
    def _():
        for chunk in range(4):
            point = iota((256, PTS), 0) + chunk * 256
            child = iota((256, PTS), 1)
            order = onehot(point == POOL * (child & 63) + (child >> 6))
            joined[chunk * 256 : (chunk + 1) * 256, :] = mm(order, children[...]).astype(BF16)


def shape(dims, dtype):
    return jax.ShapeDtypeStruct(dims, dtype)


def whole(dims):
    zeros = (0,) * len(dims)
    return pl.BlockSpec(dims, lambda *_: zeros)


def layer(dims, which):
    index = (which,) + (0,) * (len(dims) - 1)
    return pl.BlockSpec((1,) + dims[1:], lambda *_: index)


def unit(which):
    return pl.BlockSpec(
        (N_BALL, 2, 64, 512), lambda i: (0, jnp.minimum(i, STEPS - 1), which, 0)
    )


def hidden_half(first, gate_up):
    if gate_up:
        return pl.BlockSpec((2, CC, 256), lambda i: (0, 0, jnp.clip(i - first, 0, 1)))
    return pl.BlockSpec((256, CC), lambda i: (jnp.clip(i - first, 0, 1), 0))


def far_halves(first):
    def half(i):
        return jnp.clip(i - first, 0, 1)

    return (
        pl.BlockSpec((N_BALL, 64, 256), lambda i: (0, 0, half(i))),
        pl.BlockSpec((N_BALL, 64, 256), lambda i: (0, 1, half(i))),
        pl.BlockSpec((N_BALL // 2, 64, 512), lambda i: (half(i), 2, 0)),
    )


def exchange(values):
    return lax.all_to_all(values, ALL, split_axis=0, concat_axis=0, tiled=True)


def other_core(values):
    return lax.ppermute(values, "core", [(0, 1), (1, 0)])


def other_z(values):
    return lax.ppermute(values, "z", [(0, 1), (1, 0), (2, 3), (3, 2)])


def far_z(values):
    return lax.ppermute(values, "z", [(0, 3), (3, 0), (1, 2), (2, 1)])


def fine(which, rows, place, slots, norm, qkv, out, gate_up, down):
    return pl.pallas_call(
        functools.partial(fine_kernel, which),
        grid=(1,),
        out_shape=shape((SLOTS, C), BF16),
        in_specs=[
            whole((SLOTS, C)),
            pl.BlockSpec((SLOTS, N_DEV), lambda i: (0, 2)),
            whole((2, PTS)),
            layer(norm.shape, which),
            layer(qkv.shape, which),
            layer(out.shape, which),
            layer(gate_up.shape, which),
            layer(down.shape, which),
        ],
        out_specs=whole((SLOTS, C)),
        scratch_shapes=[pltpu.VMEM((8, SLOTS), I32), pltpu.VMEM((PTS, C), BF16)],
        compiler_params=params(),
        cost_estimate=pl.CostEstimate(flops=8 * 10**9, bytes_accessed=4 * 2**20, transcendentals=0),
        name=f"fine_block_{which}",
    )(rows, place, slots, norm, qkv, out, gate_up, down)


def body(
    points,
    tree_slot,
    rotated_slot,
    fine_norm,
    fine_qkv,
    fine_out,
    fine_gate_up,
    fine_down,
    pool_weight,
    coarse_norm,
    coarse_qkv,
    coarse_out,
    coarse_gate_up,
    coarse_down,
    unpool_weight,
):
    mlp_piece, piece = pl.pallas_call(
        slice_kernel,
        grid_spec=pltpu.PrefetchScalarGridSpec(
            num_scalar_prefetch=1,
            grid=(1,),
            in_specs=[
                pl.BlockSpec((2, 64, 512), lambda i, at: (0, at[0], 0)),
                pl.BlockSpec((32, CC), lambda i, at: (at[0], 0)),
                pl.BlockSpec((32, CC), lambda i, at: (at[0], 0)),
                pl.BlockSpec((64, 512), lambda i, at: (at[0], 0)),
                pl.BlockSpec((3, 64, 128), lambda i, at: (0, at[0], 0)),
                pl.BlockSpec((64, 128), lambda i, at: (at[0] // 8, at[0] % 8)),
            ],
            out_specs=(pl.BlockSpec((192, 512), lambda i, at: (0, 0)),) * 2,
        ),
        out_shape=(shape((192, 512), BF16),) * 2,
        compiler_params=params(),
        name="cut",
    )(
        lax.axis_index("ball").reshape(1),
        coarse_gate_up,
        coarse_down,
        pool_weight,
        unpool_weight,
        coarse_qkv,
        coarse_out,
    )
    weights = lax.all_gather(piece, ALL).reshape(N_BALL, N_HID, 192, 512)

    send, slots = pl.pallas_call(
        prep_kernel,
        out_shape=(shape((SLOTS, C + N_DEV), BF16), shape((2, PTS), I32)),
        compiler_params=params(),
        cost_estimate=pl.CostEstimate(flops=6 * 10**9, bytes_accessed=2 * 2**20, transcendentals=0),
        name="prep",
    )(points, tree_slot.reshape(1, PTS), rotated_slot.reshape(1, PTS))
    far_piece, send = lax.optimization_barrier((far_z(mlp_piece), send))
    far_mlp = lax.all_gather(far_piece, "ball")
    first = exchange(send)
    fine_weights = (fine_norm, fine_qkv, fine_out, fine_gate_up, fine_down)
    rows = exchange(fine(0, first, first, slots, *fine_weights))
    returned = exchange(fine(1, rows, first, slots, *fine_weights))

    block_two, coarse = pl.pallas_call(
        pool_kernel,
        grid=(STEPS,),
        out_shape=(shape((PTS, C), BF16), shape((CROWS, CC), BF16)),
        in_specs=[whole((SLOTS, C)), whole((2, PTS)), unit(0)],
        out_specs=(pl.BlockSpec((256, C), lambda i: (i, 0)), whole((CROWS, CC))),
        scratch_shapes=[pltpu.VMEM((CROWS, CC), F32)],
        compiler_params=params(),
        name="pool",
    )(returned, slots, weights)

    from_z = other_z(coarse)
    rows_64 = whole((CROWS, CC))
    rows_256 = whole((4 * CROWS, CC))
    mid, normed, partial = pl.pallas_call(
        attn_kernel,
        grid=(STEPS + 2,),
        out_shape=(
            shape((CROWS, CC), BF16),
            shape((4 * CROWS, CC), BF16),
            shape((4 * CROWS, CC), F32),
        ),
        in_specs=[
            rows_64,
            rows_64,
            rows_64,
            rows_64,
            whole((2, CC)),
            unit(2),
            hidden_half(STEPS, True),
            hidden_half(STEPS, False),
        ],
        out_specs=(rows_64, rows_256, rows_256),
        scratch_shapes=[
            pltpu.VMEM((4 * CROWS, CC), BF16),
            pltpu.VMEM((4 * CROWS, CC), F32),
            pltpu.VMEM((256, CC), BF16),
        ],
        compiler_params=params(),
        name="attn",
    )(
        coarse,
        from_z,
        other_core(coarse),
        other_core(from_z),
        coarse_norm,
        weights,
        coarse_gate_up,
        coarse_down,
    )

    kept, kept_z, sent = pl.pallas_call(
        mlp_kernel,
        grid=(2,),
        out_shape=(
            shape((CROWS, CC), F32),
            shape((CROWS, CC), F32),
            shape((2 * CROWS, CC), BF16),
        ),
        in_specs=[rows_256, rows_256, *far_halves(0)],
        out_specs=(rows_64, rows_64, whole((2 * CROWS, CC))),
        scratch_shapes=[pltpu.VMEM((4 * CROWS, CC), F32)],
        compiler_params=params(),
        name="mlp",
    )(normed, partial, far_mlp, far_mlp, far_mlp)

    got = other_core(sent)
    got_z = other_z((kept_z + got[CROWS:].astype(F32)).astype(BF16))
    return pl.pallas_call(
        unpool_kernel,
        grid=(STEPS,),
        out_shape=shape((PTS, C), BF16),
        in_specs=[
            rows_64,
            rows_64,
            rows_64,
            rows_64,
            unit(1),
            pl.BlockSpec((256, C), lambda i: (i, 0)),
        ],
        out_specs=whole((PTS, C)),
        scratch_shapes=[pltpu.VMEM((CROWS, CC), BF16), pltpu.VMEM((PTS, C), BF16)],
        compiler_params=params(),
        name="unpool",
    )(mid, kept, got, got_z, weights, block_two)


def solution(mesh):
    split = Mesh(mesh.devices.reshape(N_BALL, N_Z, 2), ALL)
    hid = ("z", "core")
    placed = (
        P(ALL, None),
        P(ALL),
        P(ALL),
        P(),
        P(),
        P(),
        P(),
        P(),
        P(hid, None),
        P(),
        P(None, None, hid),
        P(hid, None),
        P(None, None, hid),
        P(hid, None),
        P(None, hid),
    )
    return jax.shard_map(
        body, mesh=split, in_specs=placed, out_specs=P(ALL, None), check_vma=False
    )
```
